256 devices in a mesh: ctx: 64 (over y, z, x_lo), ch: 4 (over x_hi, core).
Axes of the slice: x: 4 (x_hi: 2, x_lo: 2; x = x_hi * 2 + x_lo), y: 4, z: 8, core: 2. Of those that a mesh axis runs over, the one named last changes fastest.
Arguments:
- base_ids: int32 [8192], P('ctx'), may hold values from 0 to 511
- base_table: bfloat16 [512, 3, 4096], P(None, None, 'ch'), may hold values from -6 to 6
- short_taps: float32 [3, 3, 4096], P(None, None, 'ch'), may hold values from -2.4 to 2.4
- mode_rates: float32 [16, 4096], P(None, 'ch'), may hold values from 3e-05 to 0.1
- mode_residues: float32 [16, 4096], P(None, 'ch'), may hold values from -1.8 to 1.8
- skip_gain: float32 [4096], P('ch'), may hold values from 0.5 to 1.5
- out_weight: bfloat16 [4096, 8192], P('ctx', 'ch'), may hold values from -0.09375 to 0.09375
Outputs:
- mixed: bfloat16 [8192, 8192], P('ctx', 'ch')
The draws below stay inside these ranges and needn't reach their ends.
All inputs are finite; a program needn't handle non-finite values.
Results may differ from the reference program's by a relative error of at most 0.013.
Values may be sent and summed in bfloat16 or wider, within the bound.
A program may use at most 128 MiB of HBM per device.

```python
import math
import jax
import jax.numpy as jnp
from jax import lax

D = 8192
VOCAB = 512
C = 4096
R = 16
SEQ = 8192


def place_ends(drawn, rng, least, high):
    index_at = [jax.random.randint(jax.random.fold_in(rng, axis), (), 0, length) for axis, length in enumerate(drawn.shape)]
    widest = drawn.shape.index(max(drawn.shape))
    neighbour = index_at[:widest] + [(index_at[widest] + 1) % drawn.shape[widest]] + index_at[widest + 1:]
    return drawn.at[tuple(index_at)].set(least).at[tuple(neighbour)].set(high)


def block_scale(own_key, dims, pieces, low, top_value):
    loudness, own = 1.0, jax.random.fold_in(own_key, 6)
    for axis_at, shards_of in pieces:
        heights = jnp.exp(jax.random.uniform(jax.random.fold_in(own, axis_at), (shards_of,), jnp.float32, low / len(pieces), top_value / len(pieces)))
        loudness = loudness * jnp.repeat(heights, dims[axis_at] // shards_of).reshape([-1 if axis == axis_at else 1 for axis in range(len(dims))])
    return loudness


def noise(own_key, extent, deviation, most, shards=(), kind=jnp.bfloat16):
    values = deviation * jax.random.normal(own_key, extent, jnp.float32)
    if shards:
        values = values * block_scale(own_key, extent, shards, -0.22, 0.18)
    return jnp.clip(values, -most, most).astype(kind)


def setup_inputs(seed: int = 0) -> dict:
    keys = jax.random.split(jax.random.key(seed), 8)
    base_ids = place_ends(jax.random.randint(keys[0], (SEQ,), 0, VOCAB), jax.random.fold_in(keys[0], 1), 0, VOCAB - 1).astype(jnp.int32)
    base_table = noise(keys[1], (VOCAB, 3, C), 1.0, 6.0, ((2, 4),))
    short_taps = noise(keys[2], (3, 3, C), 0.6, 2.4, ((2, 4),), jnp.float32)
    mode_rates = jnp.clip(jnp.exp(math.log(0.1) - 8.111728 * jax.random.uniform(keys[3], (R, C), jnp.float32) ** block_scale(keys[3], (R, C), ((1, 4),), -0.2, 0.2)), 2.9999999242136255e-05, 0.1)
    mode_residues = noise(keys[4], (R, C), 0.3, 1.8, ((1, 4),), jnp.float32)
    skip_gain = jnp.clip(0.5 + 1.0 * jax.random.uniform(keys[5], (C,), jnp.float32) ** block_scale(keys[5], (C,), ((0, 4),), -0.2, 0.2), 0.5, 1.5)
    out_weight = noise(keys[6], (C, D), C ** -0.5, 0.09375, ((0, 64), (1, 4)))
    return {"base_ids": base_ids, "base_table": base_table, "short_taps": short_taps, "mode_rates": mode_rates, "mode_residues": mode_residues, "skip_gain": skip_gain, "out_weight": out_weight}


def long_conv(values, rates, residues):
    group = min(C, 256)
    count = C // group
    grouped = values.T.reshape(count, group, SEQ)
    rate_groups = rates.reshape(R, count, group).transpose(1, 0, 2)
    coef_groups = (residues * jnp.sqrt(2.0 * rates)).reshape(R, count, group).transpose(1, 0, 2)
    length = 2 * SEQ

    def one_group(operands):
        signal, rate_part, coef_part = operands
        lags = jnp.arange(SEQ).astype(jnp.float32)
        filt = jnp.zeros((group, SEQ), jnp.float32)
        for mode in range(R):
            filt = filt + coef_part[mode][:, None] * jnp.exp(-rate_part[mode][:, None] * lags[None, :])
        spectrum = jnp.fft.rfft(signal, length) * jnp.fft.rfft(filt, length)
        return jnp.fft.irfft(spectrum, length)[:, :SEQ]
    result = lax.map(one_group, (grouped, rate_groups, coef_groups))
    return result.reshape(C, SEQ).T

def reference(base_ids, base_table, short_taps, mode_rates, mode_residues, skip_gain, out_weight):
    rows = jnp.take(base_table, base_ids, axis=0).astype(jnp.float32)
    padded = jnp.concatenate([jnp.zeros((2, 3, C), jnp.float32), rows], axis=0)
    feat = short_taps[0] * padded[2:] + short_taps[1] * padded[1:-1] + short_taps[2] * padded[:-2]
    query = feat[:, 0]
    keyed = feat[:, 1]
    valued = feat[:, 2]
    product = (keyed * valued).astype(jnp.bfloat16)
    product_f = product.astype(jnp.float32)
    convolved = long_conv(product_f, mode_rates, mode_residues)
    gated = (query * (convolved + skip_gain * product_f)).astype(jnp.bfloat16)
    return jnp.dot(gated, out_weight, preferred_element_type=jnp.float32).astype(jnp.bfloat16)
```

```python
import functools
import jax
import jax.numpy as jnp
from jax import lax
from jax.experimental import pallas as pl
from jax.experimental.pallas import tpu as pltpu
from jax.sharding import PartitionSpec as P

MESH = pl.DeviceIdType.MESH
NY, NZ, NX, NCH = 4, 8, 2, 4
PLANE = NZ * NX
T = 128
CL = 1024
LT = CL // 128
R = 16
KS = 64
NL = 2048
NCHUNK = 8
CW = NL // NCHUNK
HW = CW // 2
PAIRED = (0, 1, 2, 3)
SHARD = (4, 5, 6, 7)
ORDER = (0, 4, 1, 5, 2, 6, 3, 7)


def right_steps(n):
    return 4 if n % 2 == 0 else 3


def left_steps(n):
    return NZ - 1 - right_steps(n)


def kernel(
    ids_ref, taps_ref, rates_ref, res_ref, skip_ref, table_hbm, w_hbm, out_ref,
    table, rows, halo_out, halo_in, q_ref, u_ref, u2d, z2d, rate_t, coef_t,
    e_out, e_in, s_out, s_in, tot_out, tot_in, ybf, ybuf, wbuf,
    o_stage, relay_in, f32_part, fin_out, fin_in,
    sem_table, sem_w, halo_s, halo_r, e_s, e_r, t_s, t_r, b_s, b_r,
    yx_s, yx_r, yc_s, yc_r, yl_s, wx_s, wx_r, wz_s, wz_r,
    rl_s, rl_r, fn_s, fn_r,
):
    f32 = jnp.float32
    i = lax.axis_index("ctx")
    c = lax.axis_index("ch")
    y = i // PLANE
    p = lax.rem(i, PLANE)
    z = p // NX
    xl = lax.rem(p, NX)

    def in_plane(q):
        return (y * PLANE + q, c)

    def at(yy, cc):
        return (yy * PLANE + p, cc)

    def rdma(src, dst, ss, rs, dev):
        return pltpu.make_async_remote_copy(
            src_ref=src, dst_ref=dst, send_sem=ss, recv_sem=rs, device_id=dev, device_id_type=MESH
        )

    bar = pltpu.get_barrier_semaphore()
    n_peers = 0
    for d in range(1, PLANE):
        pl.semaphore_signal(bar, inc=1, device_id=in_plane(lax.rem(p + d, PLANE)), device_id_type=MESH)
        n_peers += 1
    for dy in range(NY):
        for dc in range(NCH):
            if dy or dc:
                pl.semaphore_signal(
                    bar, inc=1, device_id=at(lax.rem(y + dy, NY), lax.rem(c + dc, NCH)), device_id_type=MESH
                )
                n_peers += 1
    nxt, prv = lax.rem(i + 1, NY * PLANE), lax.rem(i + NY * PLANE - 1, NY * PLANE)
    for other in (nxt, prv):
        pl.semaphore_signal(bar, inc=1, device_id=(other, c), device_id_type=MESH)
        n_peers += 1

    def table_copy(w):
        return pltpu.make_async_copy(table_hbm.at[w], table.at[w], sem_table.at[w])

    own_row = pl.multiple_of(p * KS, KS)

    def w_copy(n):
        return pltpu.make_async_copy(
            w_hbm.at[:, pl.ds(n * CW, CW)], wbuf.at[n, pl.ds(own_row, KS), :], sem_w.at[n]
        )

    for w in (1, 2, 0):
        table_copy(w).start()
    for n in ORDER:
        w_copy(n).start()

    for lt in range(LT):
        cols = slice(lt * 128, (lt + 1) * 128)
        rt = rates_ref[:, cols]
        rate_t[pl.ds(lt, R, stride=LT), :] = rt
        coef_t[pl.ds(lt, R, stride=LT), :] = res_ref[:, cols] * jnp.sqrt(2.0 * rt)

    ids_f = jnp.broadcast_to(ids_ref[...].astype(f32), (T, T))
    ids_col = jnp.transpose(ids_f)
    lane = lax.broadcasted_iota(jnp.int32, (T, T), 1).astype(f32)
    onehot = jnp.concatenate(
        [jnp.where(ids_col == lane + float(128 * j), 1.0, 0.0).astype(jnp.bfloat16) for j in range(4)], axis=1
    )
    for w in (1, 2, 0):
        table_copy(w).wait()
        for h in range(4):
            cols = slice(h * 256, (h + 1) * 256)
            rows[w, 8:, cols] = jnp.dot(onehot, table[w, :, cols], preferred_element_type=f32)
        halo_out[w, :, :] = rows[w, 8 + T - 2:, :]

    pl.semaphore_wait(bar, n_peers)

    halo = rdma(halo_out, halo_in, halo_s, halo_r, (nxt, c))
    halo.start()

    partner = in_plane(p + 1 - 2 * xl)
    zr = in_plane(lax.rem(z + 1, NZ) * NX + xl)
    zl = in_plane(lax.rem(z + NZ - 1, NZ) * NX + xl)

    def w_rows(n, zz):
        if n in PAIRED:
            return wbuf.at[n, pl.ds(pl.multiple_of(zz * (2 * KS), 2 * KS), 2 * KS), :]
        return wbuf.at[n, pl.ds(pl.multiple_of(zz * (2 * KS) + xl * KS, KS), KS), :]

    def zat(d):
        return lax.rem(z + d + NZ, NZ)

    def w_x(n, zz):
        ref = wbuf.at[n, pl.ds(pl.multiple_of(zz * (2 * KS) + xl * KS, KS), KS), :]
        return ref

    def x_copy(n, d):
        ref = w_x(n, zat(d))
        return rdma(ref, ref, wx_s.at[n, d % NZ], wx_r.at[n, d % NZ], partner)

    def ring(n, direction, s):
        ref = w_rows(n, zat(-s if direction == 0 else s))
        return rdma(ref, ref, wz_s.at[n, direction, s], wz_r.at[n, direction, s], zr if direction == 0 else zl)

    for n in ORDER:
        w_copy(n).wait()
        if n in PAIRED:
            x_copy(n, 0).start()

    def w_op(n, s):
        steps = (right_steps(n), left_steps(n))
        if s == 0:
            if n in PAIRED:
                x_copy(n, 0).wait_recv()
            for direction in (0, 1):
                ring(n, direction, 0).start()
            if n not in PAIRED:
                x_copy(n, 0).start()
            return
        for direction in (0, 1):
            if s - 1 < steps[direction]:
                ring(n, direction, s - 1).wait_recv()
                if s < steps[direction]:
                    ring(n, direction, s).start()
                if n not in PAIRED:
                    x_copy(n, -s if direction == 0 else s).start()

    def w_done(n):
        if n not in PAIRED:
            for d in range(NZ):
                x_copy(n, d).wait_recv()

    ops = sorted(
        [(2 * (n % 4) + s, n % 4, n, s) for n in ORDER for s in range(5)]
    )
    ops = [(n, s) for _, _, n, s in ops]
    state = {"next": 0}

    def advance(upto):
        while state["next"] < len(ops) and upto(state["next"], ops[state["next"]]):
            w_op(*ops[state["next"]])
            state["next"] += 1

    def advance_to(k):
        advance(lambda idx, op: idx < k)

    def features(t0, n):
        for lt in range(LT):
            cols = slice(lt * 128, (lt + 1) * 128)
            feat = []
            for w in range(3):
                acc = taps_ref[0, w:w + 1, cols] * rows[w, 8 + t0:8 + t0 + n, cols]
                acc += taps_ref[1, w:w + 1, cols] * rows[w, 7 + t0:7 + t0 + n, cols]
                acc += taps_ref[2, w:w + 1, cols] * rows[w, 6 + t0:6 + t0 + n, cols]
                feat.append(acc)
            q_ref[t0:t0 + n, cols] = feat[0]
            u = (feat[1] * feat[2]).astype(jnp.bfloat16).astype(f32)
            u_ref[t0:t0 + n, cols] = u
            u2d[pl.ds(t0 * LT + lt, n, stride=LT), :] = u

    features(8, T - 8)

    rate = [rate_t[r * LT:(r + 1) * LT, :] for r in range(R)]
    decay = [jnp.exp(-v) for v in rate]

    def scan_states(lo, hi, init):
        def step(b, carry):
            s = list(carry)
            for k in range(8):
                u = u2d[pl.ds(pl.multiple_of((b * 8 + k) * LT, LT), LT), :]
                s = [s[r] * decay[r] + u for r in range(R)]
            return tuple(s)

        return lax.fori_loop(lo, hi, step, init)

    zero = jnp.zeros((LT, 128), f32)
    tail = scan_states(1, T // 8, (zero,) * R)
    for r in range(R):
        e_out[r] = tail[r]

    halo.wait_recv()
    keep = jnp.where(i == 0, 0.0, 1.0).astype(f32)
    for w in range(3):
        rows[w, 6:8, :] = halo_in[w, :, :] * keep
    features(0, 8)
    head = scan_states(0, 1, (zero,) * R)
    for r in range(R):
        e_out[r] = e_out[r] + jnp.exp(-float(T - 8) * rate[r]) * head[r]

    def e_copy(d):
        to = lax.rem(p + d, PLANE)
        return rdma(e_out.at[to], e_in.at[p], e_s.at[d], e_r.at[p], in_plane(to))

    def e_from(d):
        frm = lax.rem(p + d, PLANE)
        return rdma(e_out.at[frm], e_in.at[frm], e_s.at[d], e_r.at[frm], in_plane(frm))

    for d in range(1, PLANE):
        e_copy(d).start()
    e_in[p] = e_out[p]
    advance_to(4)
    for d in range(1, PLANE):
        e_from(d).wait_recv()

    my_rate = rate_t[pl.ds(pl.multiple_of(p * LT, LT), LT), :]
    dev_decay = jnp.exp(-float(T) * my_rate)
    pref = zero
    prefs = []
    for j in range(PLANE):
        prefs.append(pref)
        pref = pref * dev_decay + e_in[j]
    tot_out[...] = pref

    def t_copy(d):
        to = lax.rem(y + d, NY)
        return rdma(tot_out, tot_in.at[y], t_s.at[d], t_r.at[y], at(to, c))

    def t_from(d):
        frm = lax.rem(y + d, NY)
        return rdma(tot_out, tot_in.at[frm], t_s.at[d], t_r.at[frm], at(frm, c))

    for d in range(1, NY):
        t_copy(d).start()
    tot_in[y] = pref
    advance_to(8)
    for d in range(1, NY):
        t_from(d).wait_recv()
    carry = zero
    for yy in range(NY - 1):
        gap = jnp.maximum(y - 1 - yy, 0).astype(f32) * float(PLANE * T)
        carry = carry + jnp.where(yy < y, jnp.exp(-gap * my_rate) * tot_in[yy], 0.0)
    for j in range(PLANE):
        s_out[j] = prefs[j] + jnp.exp(-float(T * j) * my_rate) * carry

    def s_copy(d):
        to = lax.rem(p + d, PLANE)
        return rdma(s_out.at[to], s_in.at[p], b_s.at[d], b_r.at[p], in_plane(to))

    def s_from(d):
        frm = lax.rem(p + d, PLANE)
        return rdma(s_out.at[frm], s_in.at[frm], b_s.at[d], b_r.at[frm], in_plane(frm))

    for d in range(1, PLANE):
        s_copy(d).start()
    s_in[p] = s_out[p]
    advance_to(12)
    for d in range(1, PLANE):
        s_from(d).wait_recv()

    coef = [coef_t[r * LT:(r + 1) * LT, :] for r in range(R)]

    def out_step(b, carry):
        s = list(carry)
        for k in range(4):
            at_t = pl.ds(pl.multiple_of((b * 4 + k) * LT, LT), LT)
            u = u2d[at_t, :]
            s = [s[r] * decay[r] + u for r in range(R)]
            terms = [s[r] * coef[r] for r in range(R)]
            while len(terms) > 1:
                terms = [terms[m] + terms[m + 1] for m in range(0, len(terms), 2)]
            z2d[at_t, :] = terms[0]
        return tuple(s)

    lax.fori_loop(0, T // 4, out_step, tuple(s_in[r] for r in range(R)))

    for lt in range(LT):
        cols = slice(lt * 128, (lt + 1) * 128)
        conv = z2d[pl.ds(lt, T, stride=LT), :]
        gated = q_ref[:, cols] * (conv + skip_ref[:, cols] * u_ref[:, cols])
        ybf[:, cols] = gated.astype(jnp.bfloat16)

    odd = lax.rem(y, 2)
    core = lax.rem(c, 2)

    def y_copy(h):
        return rdma(ybf, ybuf.at[y], yx_s.at[h], yx_r.at[y], at(c, 2 * h + odd))

    def y_own():
        return pltpu.make_async_copy(ybf, ybuf.at[y], yl_s)

    def is_self(h):
        return jnp.logical_and(y == c, c // 2 == h)

    for h in range(2):
        @pl.when(jnp.logical_not(is_self(h)))
        def _():
            y_copy(h).start()

    mine = y == c

    @pl.when(mine)
    def _():
        y_own().start()
        y_own().wait()

    advance_to(16)
    sib = at(y, c + 1 - 2 * core)

    def y_cross(k):
        slot = 2 * k + core
        return rdma(ybuf.at[slot], ybuf.at[slot], yc_s.at[k], yc_r.at[slot], sib)

    def y_cross_from(k):
        slot = 2 * k + 1 - core
        return rdma(ybuf.at[slot], ybuf.at[slot], yc_s.at[k], yc_r.at[slot], sib)

    for k in range(2):
        slot = 2 * k + core

        @pl.when(jnp.logical_not(jnp.logical_and(slot == y, c == y)))
        def _():
            rdma(ybf, ybuf.at[slot], yx_s.at[k], yx_r.at[slot], at(slot, y)).wait_recv()

        y_cross(k).start()
    for k in range(2):
        y_cross_from(k).wait_recv()

    yr, yl = at(lax.rem(y + 1, NY), c), at(lax.rem(y + NY - 1, NY), c)
    A, B = slice(0, HW), slice(HW, CW)

    def relay(n, side):
        return rdma(o_stage.at[n, side], relay_in.at[n, side], rl_s.at[n, side], rl_r.at[n, side], (yr, yl)[side])

    def final(n, side):
        return rdma(fin_out.at[n, side], fin_in.at[n, side], fn_s.at[n, side], fn_r.at[n, side], (yr, yl)[side])

    def product(n, d):
        block = ybuf[lax.rem(y + d, NY)]
        return jnp.dot(block, wbuf[n], preferred_element_type=f32)

    def stage1(n):
        advance(lambda idx, op: any(m == n for m, _ in ops[idx:]))
        w_done(n)
        far = product(n, 2)
        o_stage[n, 0] = far[:, A].astype(jnp.bfloat16)
        o_stage[n, 1] = far[:, B].astype(jnp.bfloat16)
        relay(n, 0).start()
        relay(n, 1).start()
        f32_part[n, 0] = product(n, 1)
        f32_part[n, 1] = product(n, 3)
        f32_part[n, 2] = product(n, 0)

    def stage2(n):
        relay(n, 0).wait_recv()
        fin_out[n, 0, :, A] = (f32_part[n, 0, :, A] + relay_in[n, 0].astype(f32)).astype(jnp.bfloat16)
        fin_out[n, 0, :, B] = f32_part[n, 0, :, B].astype(jnp.bfloat16)
        final(n, 0).start()
        relay(n, 1).wait_recv()
        fin_out[n, 1, :, A] = f32_part[n, 1, :, A].astype(jnp.bfloat16)
        fin_out[n, 1, :, B] = (f32_part[n, 1, :, B] + relay_in[n, 1].astype(f32)).astype(jnp.bfloat16)
        final(n, 1).start()

    def stage3(n):
        final(n, 0).wait_recv()
        final(n, 1).wait_recv()
        total = f32_part[n, 2] + fin_in[n, 0].astype(f32) + fin_in[n, 1].astype(f32)
        out_ref[:, n * CW:(n + 1) * CW] = total.astype(jnp.bfloat16)

    for k, n in enumerate(ORDER):
        stage1(n)
        if k >= 1:
            stage2(ORDER[k - 1])
        if k >= 3:
            stage3(ORDER[k - 3])
    stage2(ORDER[-1])
    for n in ORDER[-3:]:
        stage3(n)

    halo.wait_send()
    for d in range(1, PLANE):
        e_copy(d).wait_send()
        s_copy(d).wait_send()
    for d in range(1, NY):
        t_copy(d).wait_send()
    for h in range(2):
        @pl.when(jnp.logical_not(is_self(h)))
        def _():
            y_copy(h).wait_send()
    for k in range(2):
        y_cross(k).wait_send()
    for n in ORDER:
        for direction, steps in ((0, right_steps(n)), (1, left_steps(n))):
            for s in range(steps):
                ring(n, direction, s).wait_send()
        if n in PAIRED:
            x_copy(n, 0).wait_send()
        else:
            for d in range(NZ):
                x_copy(n, d).wait_send()
        for side in range(2):
            relay(n, side).wait_send()
            final(n, side).wait_send()


def body(base_ids, base_table, short_taps, mode_rates, mode_residues, skip_gain, out_weight):
    f32, bf = jnp.float32, jnp.bfloat16
    table = jnp.transpose(base_table, (1, 0, 2))
    vmem = pl.BlockSpec(memory_space=pltpu.VMEM)
    hbm = pl.BlockSpec(memory_space=pl.ANY)
    dma = pltpu.SemaphoreType.DMA
    scratch = [
        pltpu.VMEM((3, 512, CL), bf),
        pltpu.VMEM((3, T + 8, CL), f32),
        pltpu.VMEM((3, 2, CL), f32),
        pltpu.VMEM((3, 2, CL), f32),
        pltpu.VMEM((T, CL), f32),
        pltpu.VMEM((T, CL), f32),
        pltpu.VMEM((T * LT, 128), f32),
        pltpu.VMEM((T * LT, 128), f32),
        pltpu.VMEM((R * LT, 128), f32),
        pltpu.VMEM((R * LT, 128), f32),
        pltpu.VMEM((R, LT, 128), f32),
        pltpu.VMEM((R, LT, 128), f32),
        pltpu.VMEM((R, LT, 128), f32),
        pltpu.VMEM((R, LT, 128), f32),
        pltpu.VMEM((LT, 128), f32),
        pltpu.VMEM((NY, LT, 128), f32),
        pltpu.VMEM((T, CL), bf),
        pltpu.VMEM((NY, T, CL), bf),
        pltpu.VMEM((NCHUNK, CL, CW), bf),
        pltpu.VMEM((NCHUNK, 2, T, HW), bf),
        pltpu.VMEM((NCHUNK, 2, T, HW), bf),
        pltpu.VMEM((NCHUNK, 3, T, CW), f32),
        pltpu.VMEM((NCHUNK, 2, T, CW), bf),
        pltpu.VMEM((NCHUNK, 2, T, CW), bf),
        dma((3,)), dma((NCHUNK,)),
        dma, dma,
        dma((PLANE,)), dma((PLANE,)),
        dma((NY,)), dma((NY,)),
        dma((PLANE,)), dma((PLANE,)),
        dma((2,)), dma((NY,)), dma((2,)), dma((NY,)), dma,
        dma((NCHUNK, NZ)), dma((NCHUNK, NZ)),
        dma((NCHUNK, 2, 4)), dma((NCHUNK, 2, 4)),
        dma((NCHUNK, 2)), dma((NCHUNK, 2)),
        dma((NCHUNK, 2)), dma((NCHUNK, 2)),
    ]
    return pl.pallas_call(
        kernel,
        out_shape=jax.ShapeDtypeStruct((T, NL), bf),
        in_specs=[vmem] * 5 + [hbm] * 2,
        out_specs=vmem,
        scratch_shapes=scratch,
        compiler_params=pltpu.CompilerParams(
            collective_id=0, has_side_effects=True, vmem_limit_bytes=56 * 2**20
        ),
        name="mixer",
    )(
        base_ids.reshape(1, T), short_taps, mode_rates, mode_residues,
        skip_gain.reshape(1, CL), table, out_weight,
    )


def solution(mesh):
    in_specs = (
        P("ctx"),
        P(None, None, "ch"),
        P(None, None, "ch"),
        P(None, "ch"),
        P(None, "ch"),
        P("ch"),
        P("ctx", "ch"),
    )
    return jax.shard_map(body, mesh=mesh, in_specs=in_specs, out_specs=P("ctx", "ch"), check_vma=False)
```

```python
import functools
import jax
import jax.numpy as jnp
from jax import lax
from jax.experimental import pallas as pl
from jax.experimental.pallas import tpu as pltpu
from jax.sharding import PartitionSpec as P

MESH = pl.DeviceIdType.MESH
NY, NZ, NX, NCH = 4, 8, 2, 4
PLANE = NZ * NX
T = 128
CL = 1024
LT = CL // 128
R = 16
KS = 64
NL = 2048
NW = 4
WW = NL // NW
PAIRED = (0, 1)
W_ORDER = (2, 3, 0, 1)
W_STOPS = (
    ((2, 0), (3, 0)),
    ((2, 1), (3, 1), (0, 0), (1, 0)),
    ((2, 2), (3, 2), (0, 1)),
    ((1, 1), (2, 3), (3, 3), (0, 2)),
    ((1, 2), (2, 4), (3, 4), (0, 3)),
    ((1, 3), (0, 4)),
    ((1, 4),),
)
NCHUNK = 8
CW = NL // NCHUNK
HW = CW // 2
PER = NCHUNK // NW
LAG2, LAG3 = 3, 6
ORDER = tuple(n * PER + k for n in W_ORDER for k in range(PER))
FAR_FIRST = tuple(sorted(range(1, PLANE), key=lambda d: abs(d - PLANE // 2)))


def right_steps(n):
    return 4 if n % 2 == 0 else 3


def left_steps(n):
    return NZ - 1 - right_steps(n)


def kernel(
    ids_hbm, taps_hbm, rates_hbm, res_hbm, skip_hbm, table_hbm, w_hbm, out_hbm,
    out_ref,     ids_ref, taps_ref, rates_ref, res_ref, skip_ref, table, rows, halo_out, halo_in, q_ref, u_ref, u2d, z2d, rate_t, coef_t,
    e_out, e_in, s_out, s_in, tot_out, tot_in, ybf, ybuf, wbuf,
    o_stage, relay_in, f32_part, fin_out, fin_in,
    sem_out, sem_in, sem_table, sem_w, halo_s, halo_r, e_s, e_r, t_s, t_r, b_s, b_r,
    yx_s, yx_r, yc_s, yc_r, yl_s, wx_s, wx_r, wz_s, wz_r,
    rl_s, rl_r, fn_s, fn_r,
):
    f32 = jnp.float32
    i = lax.axis_index("ctx")
    c = lax.axis_index("ch")
    y = i // PLANE
    p = lax.rem(i, PLANE)
    z = p // NX
    xl = lax.rem(p, NX)

    def in_plane(q):
        return (y * PLANE + q, c)

    def at(yy, cc):
        return (yy * PLANE + p, cc)

    def rdma(src, dst, ss, rs, dev):
        return pltpu.make_async_remote_copy(
            src_ref=src, dst_ref=dst, send_sem=ss, recv_sem=rs, device_id=dev, device_id_type=MESH
        )

    bar = pltpu.get_barrier_semaphore()
    n_peers = 0
    for d in FAR_FIRST:
        pl.semaphore_signal(bar, inc=1, device_id=in_plane(lax.rem(p + d, PLANE)), device_id_type=MESH)
        n_peers += 1
    for dy in range(NY):
        for dc in range(NCH):
            if dy or dc:
                pl.semaphore_signal(
                    bar, inc=1, device_id=at(lax.rem(y + dy, NY), lax.rem(c + dc, NCH)), device_id_type=MESH
                )
                n_peers += 1
    nxt, prv = lax.rem(i + 1, NY * PLANE), lax.rem(i + NY * PLANE - 1, NY * PLANE)
    for other in (nxt, prv):
        pl.semaphore_signal(bar, inc=1, device_id=(other, c), device_id_type=MESH)
        n_peers += 1

    def table_copy(w):
        return pltpu.make_async_copy(table_hbm.at[w], table.at[w], sem_table.at[w])

    own_row = pl.multiple_of(p * KS, KS)

    def w_copy(n):
        return pltpu.make_async_copy(
            w_hbm.at[:, pl.ds(n * WW, WW)], wbuf.at[n, pl.ds(own_row, KS), :], sem_w.at[n]
        )

    small = [
        pltpu.make_async_copy(src, dst, sem_in.at[k])
        for k, (src, dst) in enumerate((
            (ids_hbm, ids_ref), (rates_hbm, rates_ref), (res_hbm, res_ref), (taps_hbm, taps_ref), (skip_hbm, skip_ref)
        ))
    ]
    for copy in small:
        copy.start()
    for w in (1, 2, 0):
        table_copy(w).start()
    for n in W_ORDER:
        w_copy(n).start()
    for copy in small:
        copy.wait()

    for lt in range(LT):
        cols = slice(lt * 128, (lt + 1) * 128)
        rt = rates_ref[:, cols]
        rate_t[pl.ds(lt, R, stride=LT), :] = rt
        coef_t[pl.ds(lt, R, stride=LT), :] = res_ref[:, cols] * jnp.sqrt(2.0 * rt)

    ids_f = jnp.broadcast_to(ids_ref[...].astype(f32), (T, T))
    ids_col = jnp.transpose(ids_f)
    lane = lax.broadcasted_iota(jnp.int32, (T, T), 1).astype(f32)
    onehot = jnp.concatenate(
        [jnp.where(ids_col == lane + float(128 * j), 1.0, 0.0).astype(jnp.bfloat16) for j in range(4)], axis=1
    )
    for w in (1, 2, 0):
        table_copy(w).wait()
        for h in range(4):
            cols = slice(h * 256, (h + 1) * 256)
            rows[w, 8:, cols] = jnp.dot(onehot, table[w, :, cols], preferred_element_type=f32)
        halo_out[w, :, :] = rows[w, 8 + T - 2:, :]

    pl.semaphore_wait(bar, n_peers)

    halo = rdma(halo_out, halo_in, halo_s, halo_r, (nxt, c))
    halo.start()

    partner = in_plane(p + 1 - 2 * xl)
    zr = in_plane(lax.rem(z + 1, NZ) * NX + xl)
    zl = in_plane(lax.rem(z + NZ - 1, NZ) * NX + xl)

    def w_rows(n, zz):
        if n in PAIRED:
            return wbuf.at[n, pl.ds(pl.multiple_of(zz * (2 * KS), 2 * KS), 2 * KS), :]
        return wbuf.at[n, pl.ds(pl.multiple_of(zz * (2 * KS) + xl * KS, KS), KS), :]

    def zat(d):
        return lax.rem(z + d + NZ, NZ)

    def w_x(n, zz):
        ref = wbuf.at[n, pl.ds(pl.multiple_of(zz * (2 * KS) + xl * KS, KS), KS), :]
        return ref

    def x_copy(n, d):
        ref = w_x(n, zat(d))
        return rdma(ref, ref, wx_s.at[n, d % NZ], wx_r.at[n, d % NZ], partner)

    def ring(n, direction, s):
        ref = w_rows(n, zat(-s if direction == 0 else s))
        return rdma(ref, ref, wz_s.at[n, direction, s], wz_r.at[n, direction, s], zr if direction == 0 else zl)

    for n in W_ORDER:
        w_copy(n).wait()
        if n in PAIRED:
            x_copy(n, 0).start()

    def w_op(n, s):
        steps = (right_steps(n), left_steps(n))
        if s == 0:
            if n in PAIRED:
                x_copy(n, 0).wait_recv()
            for direction in (0, 1):
                ring(n, direction, 0).start()
            if n not in PAIRED:
                x_copy(n, 0).start()
            return
        for direction in (0, 1):
            if s - 1 < steps[direction]:
                ring(n, direction, s - 1).wait_recv()
                if s < steps[direction]:
                    ring(n, direction, s).start()
                if n not in PAIRED:
                    x_copy(n, -s if direction == 0 else s).start()

    def w_done(n):
        if n not in PAIRED:
            for d in range(NZ):
                x_copy(n, d).wait_recv()

    ops = [op for stop in W_STOPS for op in stop]
    counts = [sum(len(stop) for stop in W_STOPS[:k + 1]) for k in range(len(W_STOPS))]
    state = {"next": 0}

    def advance(upto):
        while state["next"] < len(ops) and upto(state["next"], ops[state["next"]]):
            w_op(*ops[state["next"]])
            state["next"] += 1

    def advance_to(stop):
        advance(lambda idx, op: idx < counts[stop])

    advance_to(0)

    def features(t0, n):
        for lt in range(LT):
            cols = slice(lt * 128, (lt + 1) * 128)
            feat = []
            for w in range(3):
                acc = taps_ref[0, w:w + 1, cols] * rows[w, 8 + t0:8 + t0 + n, cols]
                acc += taps_ref[1, w:w + 1, cols] * rows[w, 7 + t0:7 + t0 + n, cols]
                acc += taps_ref[2, w:w + 1, cols] * rows[w, 6 + t0:6 + t0 + n, cols]
                feat.append(acc)
            q_ref[t0:t0 + n, cols] = feat[0]
            u = (feat[1] * feat[2]).astype(jnp.bfloat16).astype(f32)
            u_ref[t0:t0 + n, cols] = u
            u2d[pl.ds(t0 * LT + lt, n, stride=LT), :] = u

    features(8, T - 8)

    rate = [rate_t[r * LT:(r + 1) * LT, :] for r in range(R)]
    decay = [jnp.exp(-v) for v in rate]

    def scan_states(lo, hi, init):
        def step(b, carry):
            s = list(carry)
            for k in range(8):
                u = u2d[pl.ds(pl.multiple_of((b * 8 + k) * LT, LT), LT), :]
                s = [s[r] * decay[r] + u for r in range(R)]
            return tuple(s)

        return lax.fori_loop(lo, hi, step, init)

    zero = jnp.zeros((LT, 128), f32)
    tail = scan_states(1, T // 8, (zero,) * R)
    for r in range(R):
        e_out[r] = tail[r]

    halo.wait_recv()
    keep = jnp.where(i == 0, 0.0, 1.0).astype(f32)
    for w in range(3):
        rows[w, 6:8, :] = halo_in[w, :, :] * keep
    features(0, 8)
    head = scan_states(0, 1, (zero,) * R)
    for r in range(R):
        e_out[r] = e_out[r] + jnp.exp(-float(T - 8) * rate[r]) * head[r]

    def e_copy(d):
        to = lax.rem(p + d, PLANE)
        return rdma(e_out.at[to], e_in.at[p], e_s.at[d], e_r.at[p], in_plane(to))

    def e_from(d):
        frm = lax.rem(p + d, PLANE)
        return rdma(e_out.at[frm], e_in.at[frm], e_s.at[d], e_r.at[frm], in_plane(frm))

    for d in FAR_FIRST:
        e_copy(d).start()
    e_in[p] = e_out[p]
    advance_to(1)
    for d in range(1, PLANE):
        e_from(d).wait_recv()

    my_rate = rate_t[pl.ds(pl.multiple_of(p * LT, LT), LT), :]
    dev_decay = jnp.exp(-float(T) * my_rate)
    pref = zero
    prefs = []
    for j in range(PLANE):
        prefs.append(pref)
        pref = pref * dev_decay + e_in[j]
    tot_out[...] = pref

    def t_copy(d):
        to = lax.rem(y + d, NY)
        return rdma(tot_out, tot_in.at[y], t_s.at[d], t_r.at[y], at(to, c))

    def t_from(d):
        frm = lax.rem(y + d, NY)
        return rdma(tot_out, tot_in.at[frm], t_s.at[d], t_r.at[frm], at(frm, c))

    for d in range(1, NY):
        t_copy(d).start()
    tot_in[y] = pref
    advance_to(2)
    for d in range(1, NY):
        t_from(d).wait_recv()
    carry = zero
    for yy in range(NY - 1):
        gap = jnp.maximum(y - 1 - yy, 0).astype(f32) * float(PLANE * T)
        carry = carry + jnp.where(yy < y, jnp.exp(-gap * my_rate) * tot_in[yy], 0.0)
    for j in range(PLANE):
        s_out[j] = prefs[j] + jnp.exp(-float(T * j) * my_rate) * carry

    def s_copy(d):
        to = lax.rem(p + d, PLANE)
        return rdma(s_out.at[to], s_in.at[p], b_s.at[d], b_r.at[p], in_plane(to))

    def s_from(d):
        frm = lax.rem(p + d, PLANE)
        return rdma(s_out.at[frm], s_in.at[frm], b_s.at[d], b_r.at[frm], in_plane(frm))

    for d in FAR_FIRST:
        s_copy(d).start()
    s_in[p] = s_out[p]
    advance_to(3)
    for d in range(1, PLANE):
        s_from(d).wait_recv()

    coef = [coef_t[r * LT:(r + 1) * LT, :] for r in range(R)]

    def out_step(b, carry):
        s = list(carry)
        for k in range(4):
            at_t = pl.ds(pl.multiple_of((b * 4 + k) * LT, LT), LT)
            u = u2d[at_t, :]
            s = [s[r] * decay[r] + u for r in range(R)]
            terms = [s[r] * coef[r] for r in range(R)]
            while len(terms) > 1:
                terms = [terms[m] + terms[m + 1] for m in range(0, len(terms), 2)]
            z2d[at_t, :] = terms[0]
        return tuple(s)

    lax.fori_loop(0, T // 4, out_step, tuple(s_in[r] for r in range(R)))

    for lt in range(LT):
        cols = slice(lt * 128, (lt + 1) * 128)
        conv = z2d[pl.ds(lt, T, stride=LT), :]
        gated = q_ref[:, cols] * (conv + skip_ref[:, cols] * u_ref[:, cols])
        ybf[:, cols] = gated.astype(jnp.bfloat16)

    odd = lax.rem(y, 2)
    core = lax.rem(c, 2)

    def y_copy(h):
        return rdma(ybf, ybuf.at[y], yx_s.at[h], yx_r.at[y], at(c, 2 * h + odd))

    def y_own():
        return pltpu.make_async_copy(ybf, ybuf.at[y], yl_s)

    def is_self(h):
        return jnp.logical_and(y == c, c // 2 == h)

    for h in range(2):
        @pl.when(jnp.logical_not(is_self(h)))
        def _():
            y_copy(h).start()

    mine = y == c

    @pl.when(mine)
    def _():
        y_own().start()
        y_own().wait()

    halo.wait_send()
    for d in range(1, PLANE):
        e_copy(d).wait_send()
        s_copy(d).wait_send()
    for d in range(1, NY):
        t_copy(d).wait_send()
    advance_to(4)
    sib = at(y, c + 1 - 2 * core)

    def y_cross(k):
        slot = 2 * k + core
        return rdma(ybuf.at[slot], ybuf.at[slot], yc_s.at[k], yc_r.at[slot], sib)

    def y_cross_from(k):
        slot = 2 * k + 1 - core
        return rdma(ybuf.at[slot], ybuf.at[slot], yc_s.at[k], yc_r.at[slot], sib)

    for k in range(2):
        slot = 2 * k + core

        @pl.when(jnp.logical_not(jnp.logical_and(slot == y, c == y)))
        def _():
            rdma(ybf, ybuf.at[slot], yx_s.at[k], yx_r.at[slot], at(slot, y)).wait_recv()

        y_cross(k).start()
    advance_to(5)
    for k in range(2):
        y_cross_from(k).wait_recv()

    yr, yl = at(lax.rem(y + 1, NY), c), at(lax.rem(y + NY - 1, NY), c)
    A, B = slice(0, HW), slice(HW, CW)

    def relay(n, side):
        return rdma(o_stage.at[n, side], relay_in.at[n, side], rl_s.at[n, side], rl_r.at[n, side], (yr, yl)[side])

    def final(n, side):
        return rdma(fin_out.at[n, side], fin_in.at[n, side], fn_s.at[n, side], fn_r.at[n, side], (yr, yl)[side])

    def out_copy(n):
        cols = pl.ds(n * CW, CW)
        return pltpu.make_async_copy(out_ref.at[:, cols], out_hbm.at[:, cols], sem_out.at[n])

    def product(n, d):
        block = ybuf[lax.rem(y + d, NY)]
        return jnp.dot(
            block, wbuf[n // PER, :, (n % PER) * CW:(n % PER + 1) * CW], preferred_element_type=f32
        )

    def stage1(n):
        wn, half = n // PER, n % PER
        if half == 0:
            advance(lambda idx, op: any(m == wn for m, _ in ops[idx:]))
            w_done(wn)
        far = product(n, 2)
        o_stage[n, 0] = far[:, A].astype(jnp.bfloat16)
        o_stage[n, 1] = far[:, B].astype(jnp.bfloat16)
        relay(n, 0).start()
        relay(n, 1).start()
        f32_part[n, 0] = product(n, 1)
        f32_part[n, 1] = product(n, 3)
        f32_part[n, 2] = product(n, 0)

    def stage2(n):
        relay(n, 0).wait_recv()
        fin_out[n, 0, :, A] = (f32_part[n, 0, :, A] + relay_in[n, 0].astype(f32)).astype(jnp.bfloat16)
        fin_out[n, 0, :, B] = f32_part[n, 0, :, B].astype(jnp.bfloat16)
        final(n, 0).start()
        relay(n, 1).wait_recv()
        fin_out[n, 1, :, A] = f32_part[n, 1, :, A].astype(jnp.bfloat16)
        fin_out[n, 1, :, B] = (f32_part[n, 1, :, B] + relay_in[n, 1].astype(f32)).astype(jnp.bfloat16)
        final(n, 1).start()

    def stage3(n):
        final(n, 0).wait_recv()
        final(n, 1).wait_recv()
        total = f32_part[n, 2] + fin_in[n, 0].astype(f32) + fin_in[n, 1].astype(f32)
        out_ref[:, n * CW:(n + 1) * CW] = total.astype(jnp.bfloat16)
        out_copy(n).start()

    def w_sent(n):
        for direction, steps in ((0, right_steps(n)), (1, left_steps(n))):
            for s in range(steps):
                ring(n, direction, s).wait_send()
        for d in range(1 if n in PAIRED else NZ):
            x_copy(n, d).wait_send()

    for k in range(NCHUNK + LAG3):
        if k < NCHUNK:
            stage1(ORDER[k])
        if 0 <= k - LAG2 < NCHUNK:
            stage2(ORDER[k - LAG2])
        if k == NCHUNK:
            for n in W_ORDER:
                w_sent(n)
        if k >= LAG3:
            stage3(ORDER[k - LAG3])

    for h in range(2):
        @pl.when(jnp.logical_not(is_self(h)))
        def _():
            y_copy(h).wait_send()
    for k in range(2):
        y_cross(k).wait_send()
    for n in ORDER:
        for side in range(2):
            relay(n, side).wait_send()
            final(n, side).wait_send()
        out_copy(n).wait()


def body(base_ids, base_table, short_taps, mode_rates, mode_residues, skip_gain, out_weight):
    f32, bf = jnp.float32, jnp.bfloat16
    table = jnp.transpose(base_table, (1, 0, 2))
    hbm = pl.BlockSpec(memory_space=pltpu.HBM)
    dma = pltpu.SemaphoreType.DMA
    scratch = [
        pltpu.VMEM((T, NL), bf),
        pltpu.VMEM((1, T), jnp.int32),
        pltpu.VMEM((3, 3, CL), f32),
        pltpu.VMEM((R, CL), f32),
        pltpu.VMEM((R, CL), f32),
        pltpu.VMEM((1, CL), f32),
        pltpu.VMEM((3, 512, CL), bf),
        pltpu.VMEM((3, T + 8, CL), f32),
        pltpu.VMEM((3, 2, CL), f32),
        pltpu.VMEM((3, 2, CL), f32),
        pltpu.VMEM((T, CL), f32),
        pltpu.VMEM((T, CL), f32),
        pltpu.VMEM((T * LT, 128), f32),
        pltpu.VMEM((T * LT, 128), f32),
        pltpu.VMEM((R * LT, 128), f32),
        pltpu.VMEM((R * LT, 128), f32),
        pltpu.VMEM((R, LT, 128), f32),
        pltpu.VMEM((R, LT, 128), f32),
        pltpu.VMEM((R, LT, 128), f32),
        pltpu.VMEM((R, LT, 128), f32),
        pltpu.VMEM((LT, 128), f32),
        pltpu.VMEM((NY, LT, 128), f32),
        pltpu.VMEM((T, CL), bf),
        pltpu.VMEM((NY, T, CL), bf),
        pltpu.VMEM((NW, CL, WW), bf),
        pltpu.VMEM((NCHUNK, 2, T, HW), bf),
        pltpu.VMEM((NCHUNK, 2, T, HW), bf),
        pltpu.VMEM((NCHUNK, 3, T, CW), f32),
        pltpu.VMEM((NCHUNK, 2, T, CW), bf),
        pltpu.VMEM((NCHUNK, 2, T, CW), bf),
        dma((NCHUNK,)), dma((5,)), dma((3,)), dma((NW,)),
        dma, dma,
        dma((PLANE,)), dma((PLANE,)),
        dma((NY,)), dma((NY,)),
        dma((PLANE,)), dma((PLANE,)),
        dma((2,)), dma((NY,)), dma((2,)), dma((NY,)), dma,
        dma((NW, NZ)), dma((NW, NZ)),
        dma((NW, 2, 4)), dma((NW, 2, 4)),
        dma((NCHUNK, 2)), dma((NCHUNK, 2)),
        dma((NCHUNK, 2)), dma((NCHUNK, 2)),
    ]
    return pl.pallas_call(
        kernel,
        out_shape=jax.ShapeDtypeStruct((T, NL), bf),
        in_specs=[hbm] * 7,
        out_specs=hbm,
        scratch_shapes=scratch,
        compiler_params=pltpu.CompilerParams(
            collective_id=0, has_side_effects=True, vmem_limit_bytes=56 * 2**20
        ),
        name="mixer",
    )(
        base_ids.reshape(1, T), short_taps, mode_rates, mode_residues,
        skip_gain.reshape(1, CL), table, out_weight,
    )


def solution(mesh):
    in_specs = (
        P("ctx"),
        P(None, None, "ch"),
        P(None, None, "ch"),
        P(None, "ch"),
        P(None, "ch"),
        P("ch"),
        P("ctx", "ch"),
    )
    return jax.shard_map(body, mesh=mesh, in_specs=in_specs, out_specs=P("ctx", "ch"), check_vma=False)
```

```python
import functools
import jax
import jax.numpy as jnp
from jax import lax
from jax.experimental import pallas as pl
from jax.experimental.pallas import tpu as pltpu
from jax.sharding import PartitionSpec as P

MESH = pl.DeviceIdType.MESH
NY, NZ, NX, NCH = 4, 8, 2, 4
PLANE = NZ * NX
T = 128
CL = 1024
LT = CL // 128
R = 16
KS = 64
NL = 2048
NW = 4
WW = NL // NW
PAIRED = (0, 1)
W_ORDER = (0, 2, 3, 1)
W_STOPS = (
    ((2, 0), (3, 0),),
    ((0, 0), (2, 1), (3, 1),),
    ((0, 1),),
    ((2, 2), (3, 2), (0, 2), (1, 0),),
    ((2, 3), (3, 3), (0, 3), (1, 1),),
    ((0, 4), (2, 4), (3, 4), (1, 2),),
)
W_ROUNDS = (
    ((1, 3),),
    (),
    ((1, 4),),
)
NCHUNK = 8
CW = NL // NCHUNK
HW = CW // 2
PER = NCHUNK // NW
LAG2, LAG3 = 3, 6
FAR_FIRST = tuple(sorted(range(1, PLANE), key=lambda d: abs(d - PLANE // 2)))


def right_steps(n):
    return 4 if n % 2 == 0 else 3


def left_steps(n):
    return NZ - 1 - right_steps(n)


def kernel(
    ids_hbm, taps_hbm, rates_hbm, res_hbm, skip_hbm, table_hbm, w_hbm, out_hbm,
    out_ref,     ids_ref, taps_ref, rates_ref, res_ref, skip_ref, table, rows, halo_out, halo_in, q_ref, u_ref, u2d, z2d, rate_t, coef_t,
    e_out, e_in, s_out, s_in, tot_out, tot_in, ybf, ybuf, wbuf,
    o_stage, relay_in, f32_part, fin_out, fin_in,
    far_sem, sem_out, sem_in, sem_table, sem_w, halo_s, halo_r, e_s, e_r, t_s, t_r, b_s, b_r,
    yx_s, yx_r, yc_s, yc_r, yl_s, wx_s, wx_r, wz_s, wz_r,
    rl_s, rl_r, fn_s, fn_r,
):
    f32 = jnp.float32
    i = lax.axis_index("ctx")
    c = lax.axis_index("ch")
    y = i // PLANE
    p = lax.rem(i, PLANE)
    z = p // NX
    xl = lax.rem(p, NX)

    def in_plane(q):
        return (y * PLANE + q, c)

    def at(yy, cc):
        return (yy * PLANE + p, cc)

    def rdma(src, dst, ss, rs, dev):
        return pltpu.make_async_remote_copy(
            src_ref=src, dst_ref=dst, send_sem=ss, recv_sem=rs, device_id=dev, device_id_type=MESH
        )

    def zdev(d):
        return in_plane(lax.rem(z + d + NZ, NZ) * NX + xl)

    nxt, prv = lax.rem(i + 1, NY * PLANE), lax.rem(i + NY * PLANE - 1, NY * PLANE)
    partner = in_plane(p + 1 - 2 * xl)
    block = [
        at(lax.rem(y + 1, NY), c), at(lax.rem(y + NY - 1, NY), c),
        at(y, c + 1 - 2 * lax.rem(c, 2)), at(y, lax.rem(c + 2, NCH)),
    ]

    def greet(sem, devices):
        for dev in devices:
            pl.semaphore_signal(sem, inc=1, device_id=dev, device_id_type=MESH)

    bar = pltpu.get_barrier_semaphore()
    near = [zdev(1), zdev(-1), partner, (nxt, c), (prv, c)] + block
    greet(bar, near)

    def table_copy(w):
        return pltpu.make_async_copy(table_hbm.at[w], table.at[w], sem_table.at[w])

    own_row = pl.multiple_of(p * KS, KS)

    def w_copy(n):
        return pltpu.make_async_copy(
            w_hbm.at[:, pl.ds(n * WW, WW)], wbuf.at[n, pl.ds(own_row, KS), :], sem_w.at[n]
        )

    small = [
        pltpu.make_async_copy(src, dst, sem_in.at[k])
        for k, (src, dst) in enumerate((
            (ids_hbm, ids_ref), (rates_hbm, rates_ref), (res_hbm, res_ref), (taps_hbm, taps_ref), (skip_hbm, skip_ref)
        ))
    ]
    for copy in small:
        copy.start()
    for w in (1, 2, 0):
        table_copy(w).start()
    for n in W_ORDER:
        w_copy(n).start()
    for copy in small:
        copy.wait()

    for lt in range(LT):
        cols = slice(lt * 128, (lt + 1) * 128)
        rt = rates_ref[:, cols]
        rate_t[pl.ds(lt, R, stride=LT), :] = rt
        coef_t[pl.ds(lt, R, stride=LT), :] = res_ref[:, cols] * jnp.sqrt(2.0 * rt)

    ids_f = jnp.broadcast_to(ids_ref[...].astype(f32), (T, T))
    ids_col = jnp.transpose(ids_f)
    lane = lax.broadcasted_iota(jnp.int32, (T, T), 1).astype(f32)
    onehot = jnp.concatenate(
        [jnp.where(ids_col == lane + float(128 * j), 1.0, 0.0).astype(jnp.bfloat16) for j in range(4)], axis=1
    )
    for w in (1, 2, 0):
        table_copy(w).wait()
        for h in range(4):
            cols = slice(h * 256, (h + 1) * 256)
            rows[w, 8:, cols] = jnp.dot(onehot, table[w, :, cols], preferred_element_type=f32)
        halo_out[w, :, :] = rows[w, 8 + T - 2:, :]

    pl.semaphore_wait(bar, len(near))
    greet(far_sem.at[0], [zdev(1), zdev(-1)])
    greet(far_sem.at[3], block)

    halo = rdma(halo_out, halo_in, halo_s, halo_r, (nxt, c))
    halo.start()

    zr = in_plane(lax.rem(z + 1, NZ) * NX + xl)
    zl = in_plane(lax.rem(z + NZ - 1, NZ) * NX + xl)

    def w_rows(n, zz):
        if n in PAIRED:
            return wbuf.at[n, pl.ds(pl.multiple_of(zz * (2 * KS), 2 * KS), 2 * KS), :]
        return wbuf.at[n, pl.ds(pl.multiple_of(zz * (2 * KS) + xl * KS, KS), KS), :]

    def zat(d):
        return lax.rem(z + d + NZ, NZ)

    def w_x(n, zz):
        ref = wbuf.at[n, pl.ds(pl.multiple_of(zz * (2 * KS) + xl * KS, KS), KS), :]
        return ref

    def x_copy(n, d):
        ref = w_x(n, zat(d))
        return rdma(ref, ref, wx_s.at[n, d % NZ], wx_r.at[n, d % NZ], partner)

    def ring(n, direction, s):
        ref = w_rows(n, zat(-s if direction == 0 else s))
        return rdma(ref, ref, wz_s.at[n, direction, s], wz_r.at[n, direction, s], zr if direction == 0 else zl)

    for n in range(NW):
        w_copy(n).wait()
        if n in PAIRED:
            x_copy(n, 0).start()

    def w_op(n, s):
        steps = (right_steps(n), left_steps(n))
        if s == 0:
            if n in PAIRED:
                x_copy(n, 0).wait_recv()
            for direction in (0, 1):
                ring(n, direction, 0).start()
            if n not in PAIRED:
                x_copy(n, 0).start()
            return
        for direction in (0, 1):
            if s - 1 < steps[direction]:
                ring(n, direction, s - 1).wait_recv()
                if s < steps[direction]:
                    ring(n, direction, s).start()
                if n not in PAIRED:
                    x_copy(n, -s if direction == 0 else s).start()

    def w_done(n):
        if n not in PAIRED:
            for d in range(NZ):
                x_copy(n, d).wait_recv()

    def advance_to(stop):
        for op in W_STOPS[stop]:
            w_op(*op)

    advance_to(0)
    pl.semaphore_wait(far_sem.at[0], 2)
    greet(far_sem.at[1], [zdev(2), zdev(-2)])

    def features(t0, n):
        for lt in range(LT):
            cols = slice(lt * 128, (lt + 1) * 128)
            feat = []
            for w in range(3):
                acc = taps_ref[0, w:w + 1, cols] * rows[w, 8 + t0:8 + t0 + n, cols]
                acc += taps_ref[1, w:w + 1, cols] * rows[w, 7 + t0:7 + t0 + n, cols]
                acc += taps_ref[2, w:w + 1, cols] * rows[w, 6 + t0:6 + t0 + n, cols]
                feat.append(acc)
            q_ref[t0:t0 + n, cols] = feat[0]
            u = (feat[1] * feat[2]).astype(jnp.bfloat16).astype(f32)
            u_ref[t0:t0 + n, cols] = u
            u2d[pl.ds(t0 * LT + lt, n, stride=LT), :] = u

    features(8, T - 8)

    rate = [rate_t[r * LT:(r + 1) * LT, :] for r in range(R)]
    decay = [jnp.exp(-v) for v in rate]

    def scan_states(lo, hi, init):
        def step(b, carry):
            s = list(carry)
            for k in range(8):
                u = u2d[pl.ds(pl.multiple_of((b * 8 + k) * LT, LT), LT), :]
                s = [s[r] * decay[r] + u for r in range(R)]
            return tuple(s)

        return lax.fori_loop(lo, hi, step, init)

    zero = jnp.zeros((LT, 128), f32)
    tail = scan_states(1, T // 8, (zero,) * R)
    for r in range(R):
        e_out[r] = tail[r]
    pl.semaphore_wait(far_sem.at[1], 2)
    greet(far_sem.at[2], [partner])
    pl.semaphore_wait(far_sem.at[3], 4)
    greet(far_sem.at[4], block)

    halo.wait_recv()
    keep = jnp.where(i == 0, 0.0, 1.0).astype(f32)
    for w in range(3):
        rows[w, 6:8, :] = halo_in[w, :, :] * keep
    features(0, 8)
    head = scan_states(0, 1, (zero,) * R)
    for r in range(R):
        e_out[r] = e_out[r] + jnp.exp(-float(T - 8) * rate[r]) * head[r]

    pl.semaphore_wait(far_sem.at[2], 1)

    def e_copy(d):
        to = lax.rem(p + d, PLANE)
        return rdma(e_out.at[to], e_in.at[p], e_s.at[d], e_r.at[p], in_plane(to))

    def e_from(d):
        frm = lax.rem(p + d, PLANE)
        return rdma(e_out.at[frm], e_in.at[frm], e_s.at[d], e_r.at[frm], in_plane(frm))

    for d in FAR_FIRST:
        e_copy(d).start()
    e_in[p] = e_out[p]
    advance_to(1)
    for d in range(1, PLANE):
        e_from(d).wait_recv()

    pl.semaphore_wait(far_sem.at[4], 4)
    greet(far_sem.at[5], block)

    my_rate = rate_t[pl.ds(pl.multiple_of(p * LT, LT), LT), :]
    dev_decay = jnp.exp(-float(T) * my_rate)
    pref = zero
    prefs = []
    for j in range(PLANE):
        prefs.append(pref)
        pref = pref * dev_decay + e_in[j]
    tot_out[...] = pref

    def t_copy(d):
        to = lax.rem(y + d, NY)
        return rdma(tot_out, tot_in.at[y], t_s.at[d], t_r.at[y], at(to, c))

    def t_from(d):
        frm = lax.rem(y + d, NY)
        return rdma(tot_out, tot_in.at[frm], t_s.at[d], t_r.at[frm], at(frm, c))

    for d in range(1, NY):
        t_copy(d).start()
    tot_in[y] = pref
    advance_to(2)
    for d in range(1, NY):
        t_from(d).wait_recv()
    carry = zero
    for yy in range(NY - 1):
        gap = jnp.maximum(y - 1 - yy, 0).astype(f32) * float(PLANE * T)
        carry = carry + jnp.where(yy < y, jnp.exp(-gap * my_rate) * tot_in[yy], 0.0)
    for j in range(PLANE):
        s_out[j] = prefs[j] + jnp.exp(-float(T * j) * my_rate) * carry

    def s_copy(d):
        to = lax.rem(p + d, PLANE)
        return rdma(s_out.at[to], s_in.at[p], b_s.at[d], b_r.at[p], in_plane(to))

    def s_from(d):
        frm = lax.rem(p + d, PLANE)
        return rdma(s_out.at[frm], s_in.at[frm], b_s.at[d], b_r.at[frm], in_plane(frm))

    for d in FAR_FIRST:
        s_copy(d).start()
    s_in[p] = s_out[p]
    advance_to(3)
    for d in range(1, PLANE):
        s_from(d).wait_recv()

    coef = [coef_t[r * LT:(r + 1) * LT, :] for r in range(R)]

    def out_step(b, carry):
        s = list(carry)
        for k in range(4):
            at_t = pl.ds(pl.multiple_of((b * 4 + k) * LT, LT), LT)
            u = u2d[at_t, :]
            s = [s[r] * decay[r] + u for r in range(R)]
            terms = [s[r] * coef[r] for r in range(R)]
            while len(terms) > 1:
                terms = [terms[m] + terms[m + 1] for m in range(0, len(terms), 2)]
            z2d[at_t, :] = terms[0]
        return tuple(s)

    lax.fori_loop(0, T // 4, out_step, tuple(s_in[r] for r in range(R)))

    for lt in range(LT):
        cols = slice(lt * 128, (lt + 1) * 128)
        conv = z2d[pl.ds(lt, T, stride=LT), :]
        gated = q_ref[:, cols] * (conv + skip_ref[:, cols] * u_ref[:, cols])
        ybf[:, cols] = gated.astype(jnp.bfloat16)

    pl.semaphore_wait(far_sem.at[5], 4)

    odd = lax.rem(y, 2)
    core = lax.rem(c, 2)

    def y_rows(slot):
        return pl.ds(pl.multiple_of(slot * T, T), T)

    def y_copy(h):
        return rdma(ybf, ybuf.at[y_rows(y)], yx_s.at[h], yx_r.at[y], at(c, 2 * h + odd))

    def y_own():
        return pltpu.make_async_copy(ybf, ybuf.at[y_rows(y)], yl_s)

    def is_self(h):
        return jnp.logical_and(y == c, c // 2 == h)

    for h in range(2):
        @pl.when(jnp.logical_not(is_self(h)))
        def _():
            y_copy(h).start()

    mine = y == c

    @pl.when(mine)
    def _():
        y_own().start()
        y_own().wait()

    halo.wait_send()
    for d in range(1, PLANE):
        e_copy(d).wait_send()
        s_copy(d).wait_send()
    for d in range(1, NY):
        t_copy(d).wait_send()
    advance_to(4)
    sib = at(y, c + 1 - 2 * core)

    def y_cross(k):
        slot = 2 * k + core
        return rdma(ybuf.at[y_rows(slot)], ybuf.at[y_rows(slot)], yc_s.at[k], yc_r.at[slot], sib)

    def y_cross_from(k):
        slot = 2 * k + 1 - core
        return rdma(ybuf.at[y_rows(slot)], ybuf.at[y_rows(slot)], yc_s.at[k], yc_r.at[slot], sib)

    for k in range(2):
        slot = 2 * k + core

        @pl.when(jnp.logical_not(jnp.logical_and(slot == y, c == y)))
        def _():
            rdma(ybf, ybuf.at[y_rows(slot)], yx_s.at[k], yx_r.at[slot], at(slot, y)).wait_recv()

        y_cross(k).start()
    advance_to(5)
    for k in range(2):
        y_cross_from(k).wait_recv()

    yr, yl = at(lax.rem(y + 1, NY), c), at(lax.rem(y + NY - 1, NY), c)
    A, B = slice(0, HW), slice(HW, CW)

    def relay(n, side):
        return rdma(o_stage.at[n, side], relay_in.at[n, side], rl_s.at[n, side], rl_r.at[n, side], (yr, yl)[side])

    def final(n, side):
        return rdma(fin_out.at[n, side], fin_in.at[n, side], fn_s.at[n, side], fn_r.at[n, side], (yr, yl)[side])

    def out_cols(n):
        return pl.ds(pl.multiple_of(n * CW, CW), CW)

    def out_copy(n):
        return pltpu.make_async_copy(out_ref.at[:, out_cols(n)], out_hbm.at[:, out_cols(n)], sem_out.at[n])

    right, far, left = lax.rem(y + 1, NY), lax.rem(y + 2, NY), lax.rem(y + 3, NY)

    def chunk(k):
        wn = sum(jnp.where(k // PER == j, m, 0) for j, m in enumerate(W_ORDER))
        return wn, wn * PER + lax.rem(k, PER)

    def stage1(k):
        wn, n = chunk(k)
        cols = pl.ds(pl.multiple_of(lax.rem(k, PER) * CW, CW), CW)
        prod = jnp.dot(ybuf[...], wbuf[wn, :, cols], preferred_element_type=f32)
        f32_part[n] = prod.reshape(NY, T, CW)
        opposite = f32_part[n, far].astype(jnp.bfloat16)
        o_stage[n, 0] = opposite[:, A]
        o_stage[n, 1] = opposite[:, B]
        relay(n, 0).start()
        relay(n, 1).start()

    def stage2(k):
        _, n = chunk(k)
        relay(n, 0).wait_recv()
        fin_out[n, 0, :, A] = (f32_part[n, right, :, A] + relay_in[n, 0].astype(f32)).astype(jnp.bfloat16)
        fin_out[n, 0, :, B] = f32_part[n, right, :, B].astype(jnp.bfloat16)
        final(n, 0).start()
        relay(n, 1).wait_recv()
        fin_out[n, 1, :, A] = f32_part[n, left, :, A].astype(jnp.bfloat16)
        fin_out[n, 1, :, B] = (f32_part[n, left, :, B] + relay_in[n, 1].astype(f32)).astype(jnp.bfloat16)
        final(n, 1).start()

    def stage3(k):
        _, n = chunk(k)
        final(n, 0).wait_recv()
        final(n, 1).wait_recv()
        total = f32_part[n, y] + fin_in[n, 0].astype(f32) + fin_in[n, 1].astype(f32)
        out_ref[:, out_cols(n)] = total.astype(jnp.bfloat16)
        out_copy(n).start()

    def w_sent(n):
        for direction, steps in ((0, right_steps(n)), (1, left_steps(n))):
            for s in range(steps):
                ring(n, direction, s).wait_send()
        for d in range(1 if n in PAIRED else NZ):
            x_copy(n, d).wait_send()

    def round_(k, carry):
        for j, wn in enumerate(W_ORDER):
            @pl.when(k == j * PER)
            def _():
                w_done(wn)

        @pl.when(k < NCHUNK)
        def _():
            stage1(k)

        for r, stop in enumerate(W_ROUNDS):
            if stop:
                @pl.when(k == r)
                def _():
                    for op in stop:
                        w_op(*op)

        @pl.when(jnp.logical_and(k >= LAG2, k < NCHUNK + LAG2))
        def _():
            stage2(k - LAG2)

        @pl.when(k >= LAG3)
        def _():
            stage3(k - LAG3)

        return carry

    lax.fori_loop(0, NCHUNK + LAG3, round_, 0)
    for n in W_ORDER:
        w_sent(n)

    for h in range(2):
        @pl.when(jnp.logical_not(is_self(h)))
        def _():
            y_copy(h).wait_send()
    for k in range(2):
        y_cross(k).wait_send()
    for n in range(NCHUNK):
        for side in range(2):
            relay(n, side).wait_send()
            final(n, side).wait_send()
        out_copy(n).wait()


def body(base_ids, base_table, short_taps, mode_rates, mode_residues, skip_gain, out_weight):
    f32, bf = jnp.float32, jnp.bfloat16
    table = jnp.transpose(base_table, (1, 0, 2))
    hbm = pl.BlockSpec(memory_space=pltpu.HBM)
    dma = pltpu.SemaphoreType.DMA
    scratch = [
        pltpu.VMEM((T, NL), bf),
        pltpu.VMEM((1, T), jnp.int32),
        pltpu.VMEM((3, 3, CL), f32),
        pltpu.VMEM((R, CL), f32),
        pltpu.VMEM((R, CL), f32),
        pltpu.VMEM((1, CL), f32),
        pltpu.VMEM((3, 512, CL), bf),
        pltpu.VMEM((3, T + 8, CL), f32),
        pltpu.VMEM((3, 2, CL), f32),
        pltpu.VMEM((3, 2, CL), f32),
        pltpu.VMEM((T, CL), f32),
        pltpu.VMEM((T, CL), f32),
        pltpu.VMEM((T * LT, 128), f32),
        pltpu.VMEM((T * LT, 128), f32),
        pltpu.VMEM((R * LT, 128), f32),
        pltpu.VMEM((R * LT, 128), f32),
        pltpu.VMEM((R, LT, 128), f32),
        pltpu.VMEM((R, LT, 128), f32),
        pltpu.VMEM((R, LT, 128), f32),
        pltpu.VMEM((R, LT, 128), f32),
        pltpu.VMEM((LT, 128), f32),
        pltpu.VMEM((NY, LT, 128), f32),
        pltpu.VMEM((T, CL), bf),
        pltpu.VMEM((NY * T, CL), bf),
        pltpu.VMEM((NW, CL, WW), bf),
        pltpu.VMEM((NCHUNK, 2, T, HW), bf),
        pltpu.VMEM((NCHUNK, 2, T, HW), bf),
        pltpu.VMEM((NCHUNK, NY, T, CW), f32),
        pltpu.VMEM((NCHUNK, 2, T, CW), bf),
        pltpu.VMEM((NCHUNK, 2, T, CW), bf),
        pltpu.SemaphoreType.REGULAR((6,)),
        dma((NCHUNK,)), dma((5,)), dma((3,)), dma((NW,)),
        dma, dma,
        dma((PLANE,)), dma((PLANE,)),
        dma((NY,)), dma((NY,)),
        dma((PLANE,)), dma((PLANE,)),
        dma((2,)), dma((NY,)), dma((2,)), dma((NY,)), dma,
        dma((NW, NZ)), dma((NW, NZ)),
        dma((NW, 2, 4)), dma((NW, 2, 4)),
        dma((NCHUNK, 2)), dma((NCHUNK, 2)),
        dma((NCHUNK, 2)), dma((NCHUNK, 2)),
    ]
    return pl.pallas_call(
        kernel,
        out_shape=jax.ShapeDtypeStruct((T, NL), bf),
        in_specs=[hbm] * 7,
        out_specs=hbm,
        scratch_shapes=scratch,
        compiler_params=pltpu.CompilerParams(
            collective_id=0, has_side_effects=True, vmem_limit_bytes=56 * 2**20
        ),
        name="mixer",
    )(
        base_ids.reshape(1, T), short_taps, mode_rates, mode_residues,
        skip_gain.reshape(1, CL), table, out_weight,
    )


def solution(mesh):
    in_specs = (
        P("ctx"),
        P(None, None, "ch"),
        P(None, None, "ch"),
        P(None, "ch"),
        P(None, "ch"),
        P("ch"),
        P("ctx", "ch"),
    )
    return jax.shard_map(body, mesh=mesh, in_specs=in_specs, out_specs=P("ctx", "ch"), check_vma=False)
```

```python
import functools
import jax
import jax.numpy as jnp
from jax import lax
from jax.experimental import pallas as pl
from jax.experimental.pallas import tpu as pltpu
from jax.sharding import PartitionSpec as P

MESH = pl.DeviceIdType.MESH
NY, NZ, NX, NCH = 4, 8, 2, 4
PLANE = NZ * NX
T = 128
CL = 1024
LT = CL // 128
R = 16
KS = 64
NL = 2048
NW = 4
WW = NL // NW
PAIRED = (0, 1)
W_ORDER = (0, 2, 3, 1)
W_STOPS = (
    ((2, 0), (3, 0),),
    ((0, 0), (2, 1), (3, 1),),
    ((0, 1),),
    ((2, 2), (3, 2), (0, 2), (1, 0),),
    ((2, 3), (3, 3), (0, 3), (1, 1),),
    ((0, 4), (2, 4), (3, 4), (1, 2),),
)
W_ROUNDS = (
    ((1, 3),),
    (),
    (),
    ((1, 4),),
    (),
    (),
)
NCHUNK = 8
CW = NL // NCHUNK
HW = CW // 2
PER = NCHUNK // NW
LAG2, LAG3 = 3, 6
FAR_FIRST = tuple(sorted(range(1, PLANE), key=lambda d: abs(d - PLANE // 2)))


def right_steps(n):
    return 4 if n % 2 == 0 else 3


def left_steps(n):
    return NZ - 1 - right_steps(n)


def kernel(
    ids_hbm, taps_hbm, rates_hbm, res_hbm, skip_hbm, table_hbm, w_hbm, out_hbm,
    out_ref,     ids_ref, taps_ref, rates_ref, res_ref, skip_ref, table, rows, halo_out, halo_in, q_ref, u_ref, u2d, z2d, rate_t, coef_t,
    e_out, e_in, s_out, s_in, tot_out, tot_in, ybf, ybuf, wbuf,
    o_stage, relay_in, f32_part, fin_out, fin_in,
    far_sem, sem_out, sem_in, sem_table, sem_w, halo_s, halo_r, e_s, e_r, t_s, t_r, b_s, b_r,
    yx_s, yx_r, yc_s, yc_r, yl_s, wx_s, wx_r, wz_s, wz_r,
    rl_s, rl_r, fn_s, fn_r,
):
    f32 = jnp.float32
    i = lax.axis_index("ctx")
    c = lax.axis_index("ch")
    y = i // PLANE
    p = lax.rem(i, PLANE)
    z = p // NX
    xl = lax.rem(p, NX)

    def in_plane(q):
        return (y * PLANE + q, c)

    def at(yy, cc):
        return (yy * PLANE + p, cc)

    def rdma(src, dst, ss, rs, dev):
        return pltpu.make_async_remote_copy(
            src_ref=src, dst_ref=dst, send_sem=ss, recv_sem=rs, device_id=dev, device_id_type=MESH
        )

    def zdev(d):
        return in_plane(lax.rem(z + d + NZ, NZ) * NX + xl)

    nxt, prv = lax.rem(i + 1, NY * PLANE), lax.rem(i + NY * PLANE - 1, NY * PLANE)
    partner = in_plane(p + 1 - 2 * xl)
    block = [
        at(lax.rem(y + 1, NY), c), at(lax.rem(y + NY - 1, NY), c),
        at(y, c + 1 - 2 * lax.rem(c, 2)), at(y, lax.rem(c + 2, NCH)),
    ]

    def greet(sem, devices):
        for dev in devices:
            pl.semaphore_signal(sem, inc=1, device_id=dev, device_id_type=MESH)

    bar = pltpu.get_barrier_semaphore()
    near = [zdev(1), zdev(-1), partner, (nxt, c), (prv, c)] + block
    greet(bar, near)

    def table_copy(w):
        return pltpu.make_async_copy(table_hbm.at[w], table.at[w], sem_table.at[w])

    own_row = pl.multiple_of(p * KS, KS)

    def w_copy(n):
        return pltpu.make_async_copy(
            w_hbm.at[:, pl.ds(n * WW, WW)], wbuf.at[n, pl.ds(own_row, KS), :], sem_w.at[n]
        )

    small = [
        pltpu.make_async_copy(src, dst, sem_in.at[k])
        for k, (src, dst) in enumerate((
            (ids_hbm, ids_ref), (rates_hbm, rates_ref), (res_hbm, res_ref), (taps_hbm, taps_ref), (skip_hbm, skip_ref)
        ))
    ]
    for copy in small:
        copy.start()
    for w in (1, 2, 0):
        table_copy(w).start()
    for n in W_ORDER:
        w_copy(n).start()
    for copy in small:
        copy.wait()

    for lt in range(LT):
        cols = slice(lt * 128, (lt + 1) * 128)
        rt = rates_ref[:, cols]
        rate_t[pl.ds(lt, R, stride=LT), :] = rt
        coef_t[pl.ds(lt, R, stride=LT), :] = res_ref[:, cols] * jnp.sqrt(2.0 * rt)

    ids_f = jnp.broadcast_to(ids_ref[...].astype(f32), (T, T))
    ids_col = jnp.transpose(ids_f)
    lane = lax.broadcasted_iota(jnp.int32, (T, T), 1).astype(f32)
    onehot = jnp.concatenate(
        [jnp.where(ids_col == lane + float(128 * j), 1.0, 0.0).astype(jnp.bfloat16) for j in range(4)], axis=1
    )
    for w in (1, 2, 0):
        table_copy(w).wait()
        for h in range(4):
            cols = slice(h * 256, (h + 1) * 256)
            rows[w, 8:, cols] = jnp.dot(onehot, table[w, :, cols], preferred_element_type=f32)
        halo_out[w, :, :] = rows[w, 8 + T - 2:, :]

    pl.semaphore_wait(bar, len(near))
    greet(far_sem.at[0], [zdev(1), zdev(-1)])
    greet(far_sem.at[3], block)

    halo = rdma(halo_out, halo_in, halo_s, halo_r, (nxt, c))
    halo.start()

    zr = in_plane(lax.rem(z + 1, NZ) * NX + xl)
    zl = in_plane(lax.rem(z + NZ - 1, NZ) * NX + xl)

    def w_rows(n, zz):
        if n in PAIRED:
            return wbuf.at[n, pl.ds(pl.multiple_of(zz * (2 * KS), 2 * KS), 2 * KS), :]
        return wbuf.at[n, pl.ds(pl.multiple_of(zz * (2 * KS) + xl * KS, KS), KS), :]

    def zat(d):
        return lax.rem(z + d + NZ, NZ)

    def w_x(n, zz):
        ref = wbuf.at[n, pl.ds(pl.multiple_of(zz * (2 * KS) + xl * KS, KS), KS), :]
        return ref

    def x_copy(n, d):
        ref = w_x(n, zat(d))
        return rdma(ref, ref, wx_s.at[n, d % NZ], wx_r.at[n, d % NZ], partner)

    def ring(n, direction, s):
        ref = w_rows(n, zat(-s if direction == 0 else s))
        return rdma(ref, ref, wz_s.at[n, direction, s], wz_r.at[n, direction, s], zr if direction == 0 else zl)

    for n in range(NW):
        w_copy(n).wait()
        if n in PAIRED:
            x_copy(n, 0).start()

    def w_op(n, s):
        steps = (right_steps(n), left_steps(n))
        if s == 0:
            if n in PAIRED:
                x_copy(n, 0).wait_recv()
            for direction in (0, 1):
                ring(n, direction, 0).start()
            if n not in PAIRED:
                x_copy(n, 0).start()
            return
        for direction in (0, 1):
            if s - 1 < steps[direction]:
                ring(n, direction, s - 1).wait_recv()
                if s < steps[direction]:
                    ring(n, direction, s).start()
                if n not in PAIRED:
                    x_copy(n, -s if direction == 0 else s).start()

    def w_done(n):
        if n not in PAIRED:
            for d in range(NZ):
                x_copy(n, d).wait_recv()

    def advance_to(stop):
        for op in W_STOPS[stop]:
            w_op(*op)

    advance_to(0)
    pl.semaphore_wait(far_sem.at[0], 2)
    greet(far_sem.at[1], [zdev(2), zdev(-2)])

    def features(t0, n):
        for lt in range(LT):
            cols = slice(lt * 128, (lt + 1) * 128)
            feat = []
            for w in range(3):
                acc = taps_ref[0, w:w + 1, cols] * rows[w, 8 + t0:8 + t0 + n, cols]
                acc += taps_ref[1, w:w + 1, cols] * rows[w, 7 + t0:7 + t0 + n, cols]
                acc += taps_ref[2, w:w + 1, cols] * rows[w, 6 + t0:6 + t0 + n, cols]
                feat.append(acc)
            q_ref[t0:t0 + n, cols] = feat[0]
            u = (feat[1] * feat[2]).astype(jnp.bfloat16).astype(f32)
            u_ref[t0:t0 + n, cols] = u
            u2d[pl.ds(t0 * LT + lt, n, stride=LT), :] = u

    features(8, T - 8)

    rate = [rate_t[r * LT:(r + 1) * LT, :] for r in range(R)]
    decay = [jnp.exp(-v) for v in rate]

    def scan_states(lo, hi, init):
        def step(b, carry):
            s = list(carry)
            for k in range(8):
                u = u2d[pl.ds(pl.multiple_of((b * 8 + k) * LT, LT), LT), :]
                s = [s[r] * decay[r] + u for r in range(R)]
            return tuple(s)

        return lax.fori_loop(lo, hi, step, init)

    zero = jnp.zeros((LT, 128), f32)
    tail = scan_states(1, T // 8, (zero,) * R)
    for r in range(R):
        e_out[r] = tail[r]
    pl.semaphore_wait(far_sem.at[1], 2)
    greet(far_sem.at[2], [partner])
    pl.semaphore_wait(far_sem.at[3], 4)
    greet(far_sem.at[4], block)

    halo.wait_recv()
    keep = jnp.where(i == 0, 0.0, 1.0).astype(f32)
    for w in range(3):
        rows[w, 6:8, :] = halo_in[w, :, :] * keep
    features(0, 8)
    head = scan_states(0, 1, (zero,) * R)
    for r in range(R):
        e_out[r] = e_out[r] + jnp.exp(-float(T - 8) * rate[r]) * head[r]

    pl.semaphore_wait(far_sem.at[2], 1)

    def e_copy(d):
        to = lax.rem(p + d, PLANE)
        return rdma(e_out.at[to], e_in.at[p], e_s.at[d], e_r.at[p], in_plane(to))

    def e_from(d):
        frm = lax.rem(p + d, PLANE)
        return rdma(e_out.at[frm], e_in.at[frm], e_s.at[d], e_r.at[frm], in_plane(frm))

    for d in FAR_FIRST:
        e_copy(d).start()
    e_in[p] = e_out[p]
    advance_to(1)
    for d in range(1, PLANE):
        e_from(d).wait_recv()

    pl.semaphore_wait(far_sem.at[4], 4)
    greet(far_sem.at[5], block)

    my_rate = rate_t[pl.ds(pl.multiple_of(p * LT, LT), LT), :]
    dev_decay = jnp.exp(-float(T) * my_rate)
    pref = zero
    prefs = []
    for j in range(PLANE):
        prefs.append(pref)
        pref = pref * dev_decay + e_in[j]
    tot_out[...] = pref

    def t_copy(d):
        to = lax.rem(y + d, NY)
        return rdma(tot_out, tot_in.at[y], t_s.at[d], t_r.at[y], at(to, c))

    def t_from(d):
        frm = lax.rem(y + d, NY)
        return rdma(tot_out, tot_in.at[frm], t_s.at[d], t_r.at[frm], at(frm, c))

    for d in range(1, NY):
        t_copy(d).start()
    tot_in[y] = pref
    advance_to(2)
    for d in range(1, NY):
        t_from(d).wait_recv()
    carry = zero
    for yy in range(NY - 1):
        gap = jnp.maximum(y - 1 - yy, 0).astype(f32) * float(PLANE * T)
        carry = carry + jnp.where(yy < y, jnp.exp(-gap * my_rate) * tot_in[yy], 0.0)
    for j in range(PLANE):
        s_out[j] = prefs[j] + jnp.exp(-float(T * j) * my_rate) * carry

    def s_copy(d):
        to = lax.rem(p + d, PLANE)
        return rdma(s_out.at[to], s_in.at[p], b_s.at[d], b_r.at[p], in_plane(to))

    def s_from(d):
        frm = lax.rem(p + d, PLANE)
        return rdma(s_out.at[frm], s_in.at[frm], b_s.at[d], b_r.at[frm], in_plane(frm))

    for d in FAR_FIRST:
        s_copy(d).start()
    s_in[p] = s_out[p]
    advance_to(3)
    for d in range(1, PLANE):
        s_from(d).wait_recv()

    coef = [coef_t[r * LT:(r + 1) * LT, :] for r in range(R)]

    def out_step(b, carry):
        s = list(carry)
        for k in range(4):
            at_t = pl.ds(pl.multiple_of((b * 4 + k) * LT, LT), LT)
            u = u2d[at_t, :]
            s = [s[r] * decay[r] + u for r in range(R)]
            terms = [s[r] * coef[r] for r in range(R)]
            while len(terms) > 1:
                terms = [terms[m] + terms[m + 1] for m in range(0, len(terms), 2)]
            z2d[at_t, :] = terms[0]
        return tuple(s)

    lax.fori_loop(0, T // 4, out_step, tuple(s_in[r] for r in range(R)))

    for lt in range(LT):
        cols = slice(lt * 128, (lt + 1) * 128)
        conv = z2d[pl.ds(lt, T, stride=LT), :]
        gated = q_ref[:, cols] * (conv + skip_ref[:, cols] * u_ref[:, cols])
        ybf[:, cols] = gated.astype(jnp.bfloat16)

    pl.semaphore_wait(far_sem.at[5], 4)

    odd = lax.rem(y, 2)
    core = lax.rem(c, 2)

    def y_rows(slot):
        return pl.ds(pl.multiple_of(slot * T, T), T)

    def y_copy(h):
        return rdma(ybf, ybuf.at[y_rows(y)], yx_s.at[h], yx_r.at[y], at(c, 2 * h + odd))

    def y_own():
        return pltpu.make_async_copy(ybf, ybuf.at[y_rows(y)], yl_s)

    def is_self(h):
        return jnp.logical_and(y == c, c // 2 == h)

    for h in range(2):
        @pl.when(jnp.logical_not(is_self(h)))
        def _():
            y_copy(h).start()

    mine = y == c

    @pl.when(mine)
    def _():
        y_own().start()
        y_own().wait()

    halo.wait_send()
    for d in range(1, PLANE):
        e_copy(d).wait_send()
        s_copy(d).wait_send()
    for d in range(1, NY):
        t_copy(d).wait_send()
    advance_to(4)
    sib = at(y, c + 1 - 2 * core)

    def y_cross(k):
        slot = 2 * k + core
        return rdma(ybuf.at[y_rows(slot)], ybuf.at[y_rows(slot)], yc_s.at[k], yc_r.at[slot], sib)

    def y_cross_from(k):
        slot = 2 * k + 1 - core
        return rdma(ybuf.at[y_rows(slot)], ybuf.at[y_rows(slot)], yc_s.at[k], yc_r.at[slot], sib)

    for k in range(2):
        slot = 2 * k + core

        @pl.when(jnp.logical_not(jnp.logical_and(slot == y, c == y)))
        def _():
            rdma(ybf, ybuf.at[y_rows(slot)], yx_s.at[k], yx_r.at[slot], at(slot, y)).wait_recv()

        y_cross(k).start()
    advance_to(5)
    for k in range(2):
        y_cross_from(k).wait_recv()

    yr, yl = at(lax.rem(y + 1, NY), c), at(lax.rem(y + NY - 1, NY), c)
    A, B = slice(0, HW), slice(HW, CW)

    def relay(n, side):
        return rdma(o_stage.at[n, side], relay_in.at[n, side], rl_s.at[n, side], rl_r.at[n, side], (yr, yl)[side])

    def final(n, side):
        return rdma(fin_out.at[n, side], fin_in.at[n, side], fn_s.at[n, side], fn_r.at[n, side], (yr, yl)[side])

    def out_cols(n):
        return pl.ds(pl.multiple_of(n * CW, CW), CW)

    def out_copy(n):
        return pltpu.make_async_copy(out_ref.at[:, out_cols(n)], out_hbm.at[:, out_cols(n)], sem_out.at[n])

    right, far, left = lax.rem(y + 1, NY), lax.rem(y + 2, NY), lax.rem(y + 3, NY)

    def chunk(k):
        wn = sum(jnp.where(k // PER == j, m, 0) for j, m in enumerate(W_ORDER))
        return wn, wn * PER + lax.rem(k, PER)

    def stage1(k):
        wn, n = chunk(k)
        cols = pl.ds(pl.multiple_of(lax.rem(k, PER) * CW, CW), CW)
        prod = jnp.dot(ybuf[...], wbuf[wn, :, cols], preferred_element_type=f32)
        f32_part[n] = prod.reshape(NY, T, CW)
        opposite = f32_part[n, far].astype(jnp.bfloat16)
        o_stage[n, 0] = opposite[:, A]
        o_stage[n, 1] = opposite[:, B]
        relay(n, 0).start()
        relay(n, 1).start()

    def stage2(k):
        _, n = chunk(k)
        relay(n, 0).wait_recv()
        fin_out[n, 0, :, A] = (f32_part[n, right, :, A] + relay_in[n, 0].astype(f32)).astype(jnp.bfloat16)
        fin_out[n, 0, :, B] = f32_part[n, right, :, B].astype(jnp.bfloat16)
        final(n, 0).start()
        relay(n, 1).wait_recv()
        fin_out[n, 1, :, A] = f32_part[n, left, :, A].astype(jnp.bfloat16)
        fin_out[n, 1, :, B] = (f32_part[n, left, :, B] + relay_in[n, 1].astype(f32)).astype(jnp.bfloat16)
        final(n, 1).start()

    def stage3(k):
        _, n = chunk(k)
        final(n, 0).wait_recv()
        final(n, 1).wait_recv()
        total = f32_part[n, y] + fin_in[n, 0].astype(f32) + fin_in[n, 1].astype(f32)
        out_ref[:, out_cols(n)] = total.astype(jnp.bfloat16)
        out_copy(n).start()

    def w_sent(n):
        for direction, steps in ((0, right_steps(n)), (1, left_steps(n))):
            for s in range(steps):
                ring(n, direction, s).wait_send()
        for d in range(1 if n in PAIRED else NZ):
            x_copy(n, d).wait_send()

    def round_(k, carry):
        for j, wn in enumerate(W_ORDER):
            @pl.when(k == j * PER)
            def _():
                w_done(wn)

        @pl.when(k < NCHUNK)
        def _():
            stage1(k)

        for r, stop in enumerate(W_ROUNDS):
            if stop:
                @pl.when(k == r)
                def _():
                    for op in stop:
                        w_op(*op)

        @pl.when(jnp.logical_and(k >= LAG2, k < NCHUNK + LAG2))
        def _():
            stage2(k - LAG2)

        @pl.when(k >= LAG3)
        def _():
            stage3(k - LAG3)

        return carry

    lax.fori_loop(0, NCHUNK + LAG3, round_, 0)
    for n in W_ORDER:
        w_sent(n)

    for h in range(2):
        @pl.when(jnp.logical_not(is_self(h)))
        def _():
            y_copy(h).wait_send()
    for k in range(2):
        y_cross(k).wait_send()
    for n in range(NCHUNK):
        for side in range(2):
            relay(n, side).wait_send()
            final(n, side).wait_send()
        out_copy(n).wait()


def body(base_ids, base_table, short_taps, mode_rates, mode_residues, skip_gain, out_weight):
    f32, bf = jnp.float32, jnp.bfloat16
    table = jnp.transpose(base_table, (1, 0, 2))
    hbm = pl.BlockSpec(memory_space=pltpu.HBM)
    dma = pltpu.SemaphoreType.DMA
    scratch = [
        pltpu.VMEM((T, NL), bf),
        pltpu.VMEM((1, T), jnp.int32),
        pltpu.VMEM((3, 3, CL), f32),
        pltpu.VMEM((R, CL), f32),
        pltpu.VMEM((R, CL), f32),
        pltpu.VMEM((1, CL), f32),
        pltpu.VMEM((3, 512, CL), bf),
        pltpu.VMEM((3, T + 8, CL), f32),
        pltpu.VMEM((3, 2, CL), f32),
        pltpu.VMEM((3, 2, CL), f32),
        pltpu.VMEM((T, CL), f32),
        pltpu.VMEM((T, CL), f32),
        pltpu.VMEM((T * LT, 128), f32),
        pltpu.VMEM((T * LT, 128), f32),
        pltpu.VMEM((R * LT, 128), f32),
        pltpu.VMEM((R * LT, 128), f32),
        pltpu.VMEM((R, LT, 128), f32),
        pltpu.VMEM((R, LT, 128), f32),
        pltpu.VMEM((R, LT, 128), f32),
        pltpu.VMEM((R, LT, 128), f32),
        pltpu.VMEM((LT, 128), f32),
        pltpu.VMEM((NY, LT, 128), f32),
        pltpu.VMEM((T, CL), bf),
        pltpu.VMEM((NY * T, CL), bf),
        pltpu.VMEM((NW, CL, WW), bf),
        pltpu.VMEM((NCHUNK, 2, T, HW), bf),
        pltpu.VMEM((NCHUNK, 2, T, HW), bf),
        pltpu.VMEM((NCHUNK, NY, T, CW), f32),
        pltpu.VMEM((NCHUNK, 2, T, CW), bf),
        pltpu.VMEM((NCHUNK, 2, T, CW), bf),
        pltpu.SemaphoreType.REGULAR((6,)),
        dma((NCHUNK,)), dma((5,)), dma((3,)), dma((NW,)),
        dma, dma,
        dma((PLANE,)), dma((PLANE,)),
        dma((NY,)), dma((NY,)),
        dma((PLANE,)), dma((PLANE,)),
        dma((2,)), dma((NY,)), dma((2,)), dma((NY,)), dma,
        dma((NW, NZ)), dma((NW, NZ)),
        dma((NW, 2, 4)), dma((NW, 2, 4)),
        dma((NCHUNK, 2)), dma((NCHUNK, 2)),
        dma((NCHUNK, 2)), dma((NCHUNK, 2)),
    ]
    return pl.pallas_call(
        kernel,
        out_shape=jax.ShapeDtypeStruct((T, NL), bf),
        in_specs=[hbm] * 7,
        out_specs=hbm,
        scratch_shapes=scratch,
        compiler_params=pltpu.CompilerParams(
            collective_id=0, has_side_effects=True, vmem_limit_bytes=56 * 2**20
        ),
        name="mixer",
    )(
        base_ids.reshape(1, T), short_taps, mode_rates, mode_residues,
        skip_gain.reshape(1, CL), table, out_weight,
    )


def solution(mesh):
    in_specs = (
        P("ctx"),
        P(None, None, "ch"),
        P(None, None, "ch"),
        P(None, "ch"),
        P(None, "ch"),
        P("ch"),
        P("ctx", "ch"),
    )
    return jax.shard_map(body, mesh=mesh, in_specs=in_specs, out_specs=P("ctx", "ch"), check_vma=False)
```

```python
import functools
import jax
import jax.numpy as jnp
from jax import lax
from jax.experimental import pallas as pl
from jax.experimental.pallas import tpu as pltpu
from jax.sharding import PartitionSpec as P

MESH = pl.DeviceIdType.MESH
NY, NZ, NX, NCH = 4, 8, 2, 4
PLANE = NZ * NX
T = 128
CL = 1024
LT = CL // 128
R = 16
KS = 64
NL = 2048
NW = 4
WW = NL // NW
PAIRED = (0, 1)
W_ORDER = (0, 2, 3, 1)
W_STOPS = (
    ((2, 0), (3, 0),),
    ((0, 0), (2, 1), (3, 1),),
    ((0, 1),),
    ((2, 2), (3, 2), (0, 2), (1, 0),),
    ((2, 3), (3, 3), (0, 3), (1, 1),),
    ((0, 4), (2, 4), (3, 4), (1, 2),),
)
W_ROUNDS = (
    ((1, 3),),
    (),
    (),
    ((1, 4),),
    (),
    (),
)
NCHUNK = 8
CW = NL // NCHUNK
HW = CW // 2
PER = NCHUNK // NW
LAG2, LAG3 = 3, 6
FAR_FIRST = tuple(sorted(range(1, PLANE), key=lambda d: abs(d - PLANE // 2)))


def right_steps(n):
    return 4 if n % 2 == 0 else 3


def left_steps(n):
    return NZ - 1 - right_steps(n)


def kernel(
    ids_hbm, taps_hbm, rates_hbm, res_hbm, skip_hbm, table_hbm, w_hbm, out_hbm,
    out_ref,     ids_ref, taps_ref, rates_ref, res_ref, skip_ref, table, rows, halo_out, halo_in, q_ref, u_ref, u2d, z2d, rate_t, coef_t,
    e_out, e_in, s_out, s_in, tot_out, tot_in, ybf, ybuf, wbuf,
    o_stage, relay_in, f32_part, fin_out, fin_in,
    far_sem, sem_out, sem_in, sem_table, sem_w, halo_s, halo_r, e_s, e_r, t_s, t_r, b_s, b_r,
    yx_s, yx_r, yc_s, yc_r, yl_s, wx_s, wx_r, wz_s, wz_r,
    rl_s, rl_r, fn_s, fn_r,
):
    f32 = jnp.float32
    i = lax.axis_index("ctx")
    c = lax.axis_index("ch")
    y = i // PLANE
    p = lax.rem(i, PLANE)
    z = p // NX
    xl = lax.rem(p, NX)

    def in_plane(q):
        return (y * PLANE + q, c)

    def at(yy, cc):
        return (yy * PLANE + p, cc)

    def rdma(src, dst, ss, rs, dev):
        return pltpu.make_async_remote_copy(
            src_ref=src, dst_ref=dst, send_sem=ss, recv_sem=rs, device_id=dev, device_id_type=MESH
        )

    def zdev(d):
        return in_plane(lax.rem(z + d + NZ, NZ) * NX + xl)

    nxt, prv = lax.rem(i + 1, NY * PLANE), lax.rem(i + NY * PLANE - 1, NY * PLANE)
    partner = in_plane(p + 1 - 2 * xl)
    block = [
        at(lax.rem(y + 1, NY), c), at(lax.rem(y + NY - 1, NY), c),
        at(y, c + 1 - 2 * lax.rem(c, 2)), at(y, lax.rem(c + 2, NCH)),
    ]

    def greet(sem, devices):
        for dev in devices:
            pl.semaphore_signal(sem, inc=1, device_id=dev, device_id_type=MESH)

    bar = pltpu.get_barrier_semaphore()
    near = [zdev(1), zdev(-1), partner, (nxt, c), (prv, c)] + block
    greet(bar, near)

    def table_copy(w):
        return pltpu.make_async_copy(table_hbm.at[w], table.at[w], sem_table.at[w])

    own_row = pl.multiple_of(p * KS, KS)

    def w_copy(n):
        return pltpu.make_async_copy(
            w_hbm.at[:, pl.ds(n * WW, WW)], wbuf.at[n, pl.ds(own_row, KS), :], sem_w.at[n]
        )

    small = [
        pltpu.make_async_copy(src, dst, sem_in.at[k])
        for k, (src, dst) in enumerate((
            (ids_hbm, ids_ref), (rates_hbm, rates_ref), (res_hbm, res_ref), (taps_hbm, taps_ref), (skip_hbm, skip_ref)
        ))
    ]
    for copy in small:
        copy.start()
    for w in (1, 2, 0):
        table_copy(w).start()
    for n in W_ORDER:
        w_copy(n).start()
    for copy in small:
        copy.wait()

    for lt in range(LT):
        cols = slice(lt * 128, (lt + 1) * 128)
        rt = rates_ref[:, cols]
        rate_t[pl.ds(lt, R, stride=LT), :] = rt
        coef_t[pl.ds(lt, R, stride=LT), :] = res_ref[:, cols] * jnp.sqrt(2.0 * rt)

    ids_f = jnp.broadcast_to(ids_ref[...].astype(f32), (T, T))
    ids_col = jnp.transpose(ids_f)
    lane = lax.broadcasted_iota(jnp.int32, (T, T), 1).astype(f32)
    onehot = jnp.concatenate(
        [jnp.where(ids_col == lane + float(128 * j), 1.0, 0.0).astype(jnp.bfloat16) for j in range(4)], axis=1
    )
    for w in (1, 2, 0):
        table_copy(w).wait()
        for h in range(4):
            cols = slice(h * 256, (h + 1) * 256)
            rows[w, 8:, cols] = jnp.dot(onehot, table[w, :, cols], preferred_element_type=f32)
        halo_out[w, :, :] = rows[w, 8 + T - 2:, :]

    pl.semaphore_wait(bar, len(near))
    greet(far_sem.at[0], [zdev(1), zdev(-1)])
    greet(far_sem.at[3], block)

    halo = rdma(halo_out, halo_in, halo_s, halo_r, (nxt, c))
    halo.start()

    zr = in_plane(lax.rem(z + 1, NZ) * NX + xl)
    zl = in_plane(lax.rem(z + NZ - 1, NZ) * NX + xl)

    def w_rows(n, zz):
        if n in PAIRED:
            return wbuf.at[n, pl.ds(pl.multiple_of(zz * (2 * KS), 2 * KS), 2 * KS), :]
        return wbuf.at[n, pl.ds(pl.multiple_of(zz * (2 * KS) + xl * KS, KS), KS), :]

    def zat(d):
        return lax.rem(z + d + NZ, NZ)

    def w_x(n, zz):
        ref = wbuf.at[n, pl.ds(pl.multiple_of(zz * (2 * KS) + xl * KS, KS), KS), :]
        return ref

    def x_copy(n, d):
        ref = w_x(n, zat(d))
        return rdma(ref, ref, wx_s.at[n, d % NZ], wx_r.at[n, d % NZ], partner)

    def ring(n, direction, s):
        ref = w_rows(n, zat(-s if direction == 0 else s))
        return rdma(ref, ref, wz_s.at[n, direction, s], wz_r.at[n, direction, s], zr if direction == 0 else zl)

    for n in range(NW):
        w_copy(n).wait()
        if n in PAIRED:
            x_copy(n, 0).start()

    def w_op(n, s):
        steps = (right_steps(n), left_steps(n))
        if s == 0:
            if n in PAIRED:
                x_copy(n, 0).wait_recv()
            for direction in (0, 1):
                ring(n, direction, 0).start()
            if n not in PAIRED:
                x_copy(n, 0).start()
            return
        for direction in (0, 1):
            if s - 1 < steps[direction]:
                ring(n, direction, s - 1).wait_recv()
                if s < steps[direction]:
                    ring(n, direction, s).start()
                if n not in PAIRED:
                    x_copy(n, -s if direction == 0 else s).start()

    def w_done(n):
        if n not in PAIRED:
            for d in range(NZ):
                x_copy(n, d).wait_recv()

    def advance_to(stop):
        for op in W_STOPS[stop]:
            w_op(*op)

    advance_to(0)
    pl.semaphore_wait(far_sem.at[0], 2)
    greet(far_sem.at[1], [zdev(2), zdev(-2)])

    def features(t0, n):
        for lt in range(LT):
            cols = slice(lt * 128, (lt + 1) * 128)
            feat = []
            for w in range(3):
                acc = taps_ref[0, w:w + 1, cols] * rows[w, 8 + t0:8 + t0 + n, cols]
                acc += taps_ref[1, w:w + 1, cols] * rows[w, 7 + t0:7 + t0 + n, cols]
                acc += taps_ref[2, w:w + 1, cols] * rows[w, 6 + t0:6 + t0 + n, cols]
                feat.append(acc)
            q_ref[t0:t0 + n, cols] = feat[0]
            u = (feat[1] * feat[2]).astype(jnp.bfloat16).astype(f32)
            u_ref[t0:t0 + n, cols] = u
            u2d[pl.ds(t0 * LT + lt, n, stride=LT), :] = u

    features(8, T - 8)

    rate = [rate_t[r * LT:(r + 1) * LT, :] for r in range(R)]
    decay = [jnp.exp(-v) for v in rate]

    def scan_states(lo, hi, init):
        def step(b, carry):
            s = list(carry)
            for k in range(8):
                u = u2d[pl.ds(pl.multiple_of((b * 8 + k) * LT, LT), LT), :]
                s = [s[r] * decay[r] + u for r in range(R)]
            return tuple(s)

        return lax.fori_loop(lo, hi, step, init)

    zero = jnp.zeros((LT, 128), f32)
    tail = scan_states(1, T // 8, (zero,) * R)
    for r in range(R):
        e_out[r] = tail[r]
    pl.semaphore_wait(far_sem.at[1], 2)
    greet(far_sem.at[2], [partner])
    pl.semaphore_wait(far_sem.at[3], 4)
    greet(far_sem.at[4], block)

    halo.wait_recv()
    keep = jnp.where(i == 0, 0.0, 1.0).astype(f32)
    for w in range(3):
        rows[w, 6:8, :] = halo_in[w, :, :] * keep
    features(0, 8)
    head = scan_states(0, 1, (zero,) * R)
    for r in range(R):
        e_out[r] = e_out[r] + jnp.exp(-float(T - 8) * rate[r]) * head[r]

    pl.semaphore_wait(far_sem.at[2], 1)

    def e_copy(d):
        to = lax.rem(p + d, PLANE)
        return rdma(e_out.at[to], e_in.at[p], e_s.at[d], e_r, in_plane(to))

    for d in FAR_FIRST:
        e_copy(d).start()
    e_in[p] = e_out[p]
    advance_to(1)
    rdma(e_out.at[pl.ds(0, R - 1)], e_in.at[pl.ds(0, R - 1)], e_s.at[0], e_r, partner).wait_recv()

    pl.semaphore_wait(far_sem.at[4], 4)
    greet(far_sem.at[5], block)

    my_rate = rate_t[pl.ds(pl.multiple_of(p * LT, LT), LT), :]
    dev_decay = jnp.exp(-float(T) * my_rate)
    pref = zero
    prefs = []
    for j in range(PLANE):
        prefs.append(pref)
        pref = pref * dev_decay + e_in[j]
    tot_out[...] = pref

    def t_copy(d):
        to = lax.rem(y + d, NY)
        return rdma(tot_out, tot_in.at[y], t_s.at[d], t_r.at[y], at(to, c))

    def t_from(d):
        frm = lax.rem(y + d, NY)
        return rdma(tot_out, tot_in.at[frm], t_s.at[d], t_r.at[frm], at(frm, c))

    for d in (2, 1, 3):
        t_copy(d).start()
    tot_in[y] = pref
    advance_to(2)
    for d in range(1, NY):
        t_from(d).wait_recv()
    carry = zero
    for yy in range(NY - 1):
        gap = jnp.maximum(y - 1 - yy, 0).astype(f32) * float(PLANE * T)
        carry = carry + jnp.where(yy < y, jnp.exp(-gap * my_rate) * tot_in[yy], 0.0)
    for j in range(PLANE):
        s_out[j] = prefs[j] + jnp.exp(-float(T * j) * my_rate) * carry

    def s_copy(d):
        to = lax.rem(p + d, PLANE)
        return rdma(s_out.at[to], s_in.at[p], b_s.at[d], b_r, in_plane(to))

    for d in FAR_FIRST:
        s_copy(d).start()
    s_in[p] = s_out[p]
    advance_to(3)
    rdma(s_out.at[pl.ds(0, R - 1)], s_in.at[pl.ds(0, R - 1)], b_s.at[0], b_r, partner).wait_recv()

    coef = [coef_t[r * LT:(r + 1) * LT, :] for r in range(R)]

    def out_step(b, carry):
        s = list(carry)
        for k in range(4):
            at_t = pl.ds(pl.multiple_of((b * 4 + k) * LT, LT), LT)
            u = u2d[at_t, :]
            s = [s[r] * decay[r] + u for r in range(R)]
            terms = [s[r] * coef[r] for r in range(R)]
            while len(terms) > 1:
                terms = [terms[m] + terms[m + 1] for m in range(0, len(terms), 2)]
            z2d[at_t, :] = terms[0]
        return tuple(s)

    lax.fori_loop(0, T // 4, out_step, tuple(s_in[r] for r in range(R)))

    for lt in range(LT):
        cols = slice(lt * 128, (lt + 1) * 128)
        conv = z2d[pl.ds(lt, T, stride=LT), :]
        gated = q_ref[:, cols] * (conv + skip_ref[:, cols] * u_ref[:, cols])
        ybf[:, cols] = gated.astype(jnp.bfloat16)

    pl.semaphore_wait(far_sem.at[5], 4)

    odd = lax.rem(y, 2)
    core = lax.rem(c, 2)

    def y_rows(slot):
        return pl.ds(pl.multiple_of(slot * T, T), T)

    def y_copy(h):
        return rdma(ybf, ybuf.at[y_rows(y)], yx_s.at[h], yx_r.at[y], at(c, 2 * h + odd))

    def y_own():
        return pltpu.make_async_copy(ybf, ybuf.at[y_rows(y)], yl_s)

    def is_self(h):
        return jnp.logical_and(y == c, c // 2 == h)

    for h in range(2):
        @pl.when(jnp.logical_not(is_self(h)))
        def _():
            y_copy(h).start()

    mine = y == c

    @pl.when(mine)
    def _():
        y_own().start()
        y_own().wait()

    halo.wait_send()
    for d in range(1, PLANE):
        e_copy(d).wait_send()
        s_copy(d).wait_send()
    for d in range(1, NY):
        t_copy(d).wait_send()
    advance_to(4)
    sib = at(y, c + 1 - 2 * core)

    def y_cross(k):
        slot = 2 * k + core
        return rdma(ybuf.at[y_rows(slot)], ybuf.at[y_rows(slot)], yc_s.at[k], yc_r.at[slot], sib)

    def y_cross_from(k):
        slot = 2 * k + 1 - core
        return rdma(ybuf.at[y_rows(slot)], ybuf.at[y_rows(slot)], yc_s.at[k], yc_r.at[slot], sib)

    for k in range(2):
        slot = 2 * k + core

        @pl.when(jnp.logical_not(jnp.logical_and(slot == y, c == y)))
        def _():
            rdma(ybf, ybuf.at[y_rows(slot)], yx_s.at[k], yx_r.at[slot], at(slot, y)).wait_recv()

        y_cross(k).start()
    advance_to(5)
    for k in range(2):
        y_cross_from(k).wait_recv()

    yr, yl = at(lax.rem(y + 1, NY), c), at(lax.rem(y + NY - 1, NY), c)
    A, B = slice(0, HW), slice(HW, CW)

    def relay(n, side):
        return rdma(o_stage.at[n, side], relay_in.at[n, side], rl_s.at[n, side], rl_r.at[n, side], (yr, yl)[side])

    def final(n, side):
        return rdma(fin_out.at[n, side], fin_in.at[n, side], fn_s.at[n, side], fn_r.at[n, side], (yr, yl)[side])

    def out_cols(n):
        return pl.ds(pl.multiple_of(n * CW, CW), CW)

    def out_copy(n):
        return pltpu.make_async_copy(out_ref.at[:, out_cols(n)], out_hbm.at[:, out_cols(n)], sem_out.at[n])

    right, far, left = lax.rem(y + 1, NY), lax.rem(y + 2, NY), lax.rem(y + 3, NY)

    def chunk(k):
        wn = sum(jnp.where(k // PER == j, m, 0) for j, m in enumerate(W_ORDER))
        return wn, wn * PER + lax.rem(k, PER)

    def stage1(k):
        wn, n = chunk(k)
        cols = pl.ds(pl.multiple_of(lax.rem(k, PER) * CW, CW), CW)
        prod = jnp.dot(ybuf[...], wbuf[wn, :, cols], preferred_element_type=f32)
        f32_part[n] = prod.reshape(NY, T, CW)
        opposite = f32_part[n, far].astype(jnp.bfloat16)
        o_stage[n, 0] = opposite[:, A]
        o_stage[n, 1] = opposite[:, B]
        relay(n, 0).start()
        relay(n, 1).start()

    def stage2(k):
        _, n = chunk(k)
        relay(n, 0).wait_recv()
        fin_out[n, 0, :, A] = (f32_part[n, right, :, A] + relay_in[n, 0].astype(f32)).astype(jnp.bfloat16)
        fin_out[n, 0, :, B] = f32_part[n, right, :, B].astype(jnp.bfloat16)
        final(n, 0).start()
        relay(n, 1).wait_recv()
        fin_out[n, 1, :, A] = f32_part[n, left, :, A].astype(jnp.bfloat16)
        fin_out[n, 1, :, B] = (f32_part[n, left, :, B] + relay_in[n, 1].astype(f32)).astype(jnp.bfloat16)
        final(n, 1).start()

    def stage3(k):
        _, n = chunk(k)
        final(n, 0).wait_recv()
        final(n, 1).wait_recv()
        total = f32_part[n, y] + fin_in[n, 0].astype(f32) + fin_in[n, 1].astype(f32)
        out_ref[:, out_cols(n)] = total.astype(jnp.bfloat16)
        out_copy(n).start()

    def w_sent(n):
        for direction, steps in ((0, right_steps(n)), (1, left_steps(n))):
            for s in range(steps):
                ring(n, direction, s).wait_send()
        for d in range(1 if n in PAIRED else NZ):
            x_copy(n, d).wait_send()

    def round_(k, carry):
        for j, wn in enumerate(W_ORDER):
            @pl.when(k == j * PER)
            def _():
                w_done(wn)

        @pl.when(k < NCHUNK)
        def _():
            stage1(k)

        for r, stop in enumerate(W_ROUNDS):
            if stop:
                @pl.when(k == r)
                def _():
                    for op in stop:
                        w_op(*op)

        @pl.when(jnp.logical_and(k >= LAG2, k < NCHUNK + LAG2))
        def _():
            stage2(k - LAG2)

        @pl.when(k >= LAG3)
        def _():
            stage3(k - LAG3)

        return carry

    lax.fori_loop(0, NCHUNK + LAG3, round_, 0)
    for n in W_ORDER:
        w_sent(n)

    for h in range(2):
        @pl.when(jnp.logical_not(is_self(h)))
        def _():
            y_copy(h).wait_send()
    for k in range(2):
        y_cross(k).wait_send()
    for n in range(NCHUNK):
        for side in range(2):
            relay(n, side).wait_send()
            final(n, side).wait_send()
        out_copy(n).wait()


def body(base_ids, base_table, short_taps, mode_rates, mode_residues, skip_gain, out_weight):
    f32, bf = jnp.float32, jnp.bfloat16
    table = jnp.transpose(base_table, (1, 0, 2))
    hbm = pl.BlockSpec(memory_space=pltpu.HBM)
    dma = pltpu.SemaphoreType.DMA
    scratch = [
        pltpu.VMEM((T, NL), bf),
        pltpu.VMEM((1, T), jnp.int32),
        pltpu.VMEM((3, 3, CL), f32),
        pltpu.VMEM((R, CL), f32),
        pltpu.VMEM((R, CL), f32),
        pltpu.VMEM((1, CL), f32),
        pltpu.VMEM((3, 512, CL), bf),
        pltpu.VMEM((3, T + 8, CL), f32),
        pltpu.VMEM((3, 2, CL), f32),
        pltpu.VMEM((3, 2, CL), f32),
        pltpu.VMEM((T, CL), f32),
        pltpu.VMEM((T, CL), f32),
        pltpu.VMEM((T * LT, 128), f32),
        pltpu.VMEM((T * LT, 128), f32),
        pltpu.VMEM((R * LT, 128), f32),
        pltpu.VMEM((R * LT, 128), f32),
        pltpu.VMEM((R, LT, 128), f32),
        pltpu.VMEM((R, LT, 128), f32),
        pltpu.VMEM((R, LT, 128), f32),
        pltpu.VMEM((R, LT, 128), f32),
        pltpu.VMEM((LT, 128), f32),
        pltpu.VMEM((NY, LT, 128), f32),
        pltpu.VMEM((T, CL), bf),
        pltpu.VMEM((NY * T, CL), bf),
        pltpu.VMEM((NW, CL, WW), bf),
        pltpu.VMEM((NCHUNK, 2, T, HW), bf),
        pltpu.VMEM((NCHUNK, 2, T, HW), bf),
        pltpu.VMEM((NCHUNK, NY, T, CW), f32),
        pltpu.VMEM((NCHUNK, 2, T, CW), bf),
        pltpu.VMEM((NCHUNK, 2, T, CW), bf),
        pltpu.SemaphoreType.REGULAR((6,)),
        dma((NCHUNK,)), dma((5,)), dma((3,)), dma((NW,)),
        dma, dma,
        dma((PLANE,)), dma,
        dma((NY,)), dma((NY,)),
        dma((PLANE,)), dma,
        dma((2,)), dma((NY,)), dma((2,)), dma((NY,)), dma,
        dma((NW, NZ)), dma((NW, NZ)),
        dma((NW, 2, 4)), dma((NW, 2, 4)),
        dma((NCHUNK, 2)), dma((NCHUNK, 2)),
        dma((NCHUNK, 2)), dma((NCHUNK, 2)),
    ]
    return pl.pallas_call(
        kernel,
        out_shape=jax.ShapeDtypeStruct((T, NL), bf),
        in_specs=[hbm] * 7,
        out_specs=hbm,
        scratch_shapes=scratch,
        compiler_params=pltpu.CompilerParams(
            collective_id=0, has_side_effects=True, vmem_limit_bytes=56 * 2**20
        ),
        name="mixer",
    )(
        base_ids.reshape(1, T), short_taps, mode_rates, mode_residues,
        skip_gain.reshape(1, CL), table, out_weight,
    )


def solution(mesh):
    in_specs = (
        P("ctx"),
        P(None, None, "ch"),
        P(None, None, "ch"),
        P(None, "ch"),
        P(None, "ch"),
        P("ch"),
        P("ctx", "ch"),
    )
    return jax.shard_map(body, mesh=mesh, in_specs=in_specs, out_specs=P("ctx", "ch"), check_vma=False)
```
